512 devices in a mesh: samp: 32 (over z, x_hi, core), box: 2 (over x_lo), rhs: 8 (over y).
Axes of the slice: x: 4 (x_hi: 2, x_lo: 2; x = x_hi * 2 + x_lo), y: 8, z: 8, core: 2. Of those that a mesh axis runs over, the one named last changes fastest.
Arguments:
- radiated: float32 [256, 16, 2, 4096], P(('box', 'samp'), 'rhs'), may hold values from -6 to 6
- low_table: float32 [320, 2, 4096], P(('box', 'rhs'), None, 'samp'), may hold values from -1.2 to 1.2
- high_table: float32 [320, 2, 16384], P(('box', 'rhs'), None, 'samp'), may hold values from -1.2 to 1.2
- low_sources: int32 [256, 16], P('box'), may hold values from 0 to 255
- low_operators: int32 [256, 16], P('box'), may hold values from 0 to 319
- high_sources: int32 [32, 16], P('box'), may hold values from 0 to 31
- high_operators: int32 [32, 16], P('box'), may hold values from 0 to 319
- stencil_index: int32 [16, 16384], replicated, may hold values from 0 to 4095, as said below
- stencil_weight: float32 [16, 16384], replicated, may hold values from -0.75 to 0.75
- shift_angle: float32 [8, 16384], replicated, may hold values from -3.140625 to 3.140625
Outputs:
- low_incoming: float32 [256, 16, 2, 4096], P('box', 'rhs', None, 'samp')
- high_incoming: float32 [32, 16, 2, 16384], P('box', 'rhs', None, 'samp')
The draws below stay inside these ranges and needn't reach their ends.
Inputs may be any that keep to these rules, and one draw needn't show every extreme that they name: stencil_index[p, j] = min(max(j // 4 + o, 0), 4095) with an offset o of -32 to 32; for every j the offset at p = 0 is -32 and at p = 15 is 32.
All inputs are finite; a program needn't handle non-finite values.
Results may differ from the reference program's by a relative error of at most 0.000071.
Values sent between devices are 32-bit elements; how exact they have to be, the bound alone decides.
No kernel may reach another device: no remote copies, remote signals or barrier semaphores. Data moves between devices by JAX's collectives and lax.ppermute only.
A program may use at most 128 MiB of HBM per device.

```python
import jax
import jax.numpy as jnp

KT = 4096
KU = 16384
HALO = 32
STEN = 16
NB_T = 256
NB_U = 32
RHS = 16
LIST = 16
NDISP = 320


def draw_stencil_index(key, part):
    key = jax.random.fold_in(key, 7)
    offsets = jax.random.randint(key, (STEN, KU), -HALO, HALO + 1)
    row = jnp.arange(STEN)[:, None]
    offsets = jnp.where(row == 0, -HALO, jnp.where(row == STEN - 1, HALO, offsets))
    centre = (jnp.arange(KU) // 4)[None, :]
    return jnp.clip(centre + offsets, 0, KT - 1).astype(jnp.int32)


def place_ends(result, stream_key, least, top_value):
    dims = result.shape
    place = [jax.random.randint(jax.random.fold_in(stream_key, axis), (), 0, dims[axis]) for axis in range(len(dims))]
    result = result.at[tuple(place)].set(least)
    longest = dims.index(max(dims))
    place[longest] = (place[longest] + 1) % dims[longest]
    return result.at[tuple(place)].set(top_value)


def shard_levels(key, shape, split, least, high):
    level = 1.0
    for dim, shards_of in split:
        draws = jax.random.uniform(jax.random.fold_in(jax.random.fold_in(key, 6), dim), (shards_of,), jnp.float32, least / len(split), high / len(split))
        level = level * jnp.repeat(jnp.exp(draws), shape[dim] // shards_of).reshape((-1,) + (1,) * (len(shape) - 1 - dim))
    return level


def bell_draw(own_key, extent, deviation, limit, cuts=(), held_as=jnp.bfloat16):
    entries = deviation * jax.random.normal(own_key, extent, jnp.float32)
    if cuts:
        entries = entries * shard_levels(own_key, extent, cuts, -0.22, 0.18)
    return jnp.clip(entries, -limit, limit).astype(held_as)


def setup_inputs(seed: int = 0) -> dict:
    key_of = jax.random.split(jax.random.key(seed), 11)
    return {
        "radiated": bell_draw(key_of[0], (NB_T, RHS, 2, KT), 1.0, 6.0, ((0, 64), (1, 8)), jnp.float32),
        "low_table": bell_draw(key_of[1], (NDISP, 2, KT), 0.18, 1.2, ((0, 16), (2, 32)), jnp.float32),
        "high_table": bell_draw(key_of[2], (NDISP, 2, KU), 0.18, 1.2, ((0, 16), (2, 32)), jnp.float32),
        "low_sources": place_ends(jax.random.randint(key_of[3], (NB_T, LIST), 0, NB_T), jax.random.fold_in(key_of[3], 1), 0, NB_T - 1).astype(jnp.int32),
        "low_operators": place_ends(jax.random.randint(key_of[4], (NB_T, LIST), 0, NDISP), jax.random.fold_in(key_of[4], 1), 0, NDISP - 1).astype(jnp.int32),
        "high_sources": place_ends(jax.random.randint(key_of[5], (NB_U, LIST), 0, NB_U), jax.random.fold_in(key_of[5], 1), 0, NB_U - 1).astype(jnp.int32),
        "high_operators": place_ends(jax.random.randint(key_of[6], (NB_U, LIST), 0, NDISP), jax.random.fold_in(key_of[6], 1), 0, NDISP - 1).astype(jnp.int32),
        "stencil_index": draw_stencil_index(jax.random.fold_in(key_of[10], 71), 0),
        "stencil_weight": bell_draw(key_of[8], (STEN, KU), (4 * STEN) ** -0.5, 0.75, (), jnp.float32),
        "shift_angle": jnp.clip(jax.random.uniform(key_of[9], (8, KU), jnp.float32, -3.140625, 3.140625), -3.140625, 3.140625),
    }


def complex_product(left_real, left_imag, right_real, right_imag):
    return (left_real * right_real - left_imag * right_imag, left_real * right_imag + left_imag * right_real)


def translate(patterns, table, sources, operators):
    summed = jnp.zeros((sources.shape[0],) + patterns.shape[1:], jnp.float32)
    for entry in range(sources.shape[1]):
        picked = patterns[sources[:, entry]]
        factor = table[operators[:, entry]]
        real_part, imag_part = complex_product(factor[:, 0][:, None], factor[:, 1][:, None], picked[:, :, 0], picked[:, :, 1])
        summed = summed + jnp.stack([real_part, imag_part], 2)
    return summed


def reference(radiated, low_table, high_table, low_sources, low_operators, high_sources, high_operators, stencil_index, stencil_weight, shift_angle):
    interpolated = jnp.zeros(radiated.shape[:3] + (KU,), jnp.float32)
    for point in range(STEN):
        interpolated = interpolated + radiated[:, :, :, stencil_index[point]] * stencil_weight[point]
    children = interpolated.reshape((NB_U, 8) + interpolated.shape[1:])
    cosine = jnp.cos(shift_angle)[None, :, None, :]
    sine_part = jnp.sin(shift_angle)[None, :, None, :]
    real_part, imag_part = complex_product(cosine, sine_part, children[:, :, :, 0], children[:, :, :, 1])
    parents = jnp.stack([jnp.sum(real_part, 1), jnp.sum(imag_part, 1)], 2)
    high_incoming = translate(parents, high_table, high_sources, high_operators)
    translated = translate(radiated, low_table, low_sources, low_operators)
    real_part, imag_part = complex_product(cosine, -sine_part, high_incoming[:, None, :, 0], high_incoming[:, None, :, 1])
    spread = jnp.stack([real_part, imag_part], 3).reshape((NB_T,) + high_incoming.shape[1:])
    anterpolated = jnp.zeros(radiated.shape, jnp.float32)
    for point in range(STEN):
        anterpolated = anterpolated.at[:, :, :, stencil_index[point]].add(spread * stencil_weight[point])
    return translated + anterpolated, high_incoming
```

```python
import jax
import jax.numpy as jnp
from jax import lax
from jax.experimental import pallas as pl
from jax.experimental.pallas import tpu as pltpu
from jax.sharding import PartitionSpec as P

F32, BF16, I32 = jnp.float32, jnp.bfloat16, jnp.int32
VMEM = pl.BlockSpec(memory_space=pltpu.VMEM)
SMEM = pl.BlockSpec(memory_space=pltpu.SMEM)
HBM = pl.BlockSpec(memory_space=pltpu.HBM)
LANES = 128
ROWS = 120
ALL_VMEM = 63 << 20
SENT = ROWS + 16


def call(kernel, ins, outs, scratch=(), flops=0, moved=0, out_place=VMEM, room=24 << 20):
    return pl.pallas_call(
        kernel,
        in_specs=list(ins),
        out_specs=[out_place] * len(outs),
        out_shape=[jax.ShapeDtypeStruct(s, d) for s, d in outs],
        scratch_shapes=list(scratch),
        compiler_params=pltpu.CompilerParams(vmem_limit_bytes=room),
        cost_estimate=pl.CostEstimate(flops=flops, bytes_accessed=moved, transcendentals=0),
    )


def halves(x):
    high = x.astype(BF16)
    return high, (x - high.astype(F32)).astype(BF16)


def row_of(shape=(8, LANES)):
    return lax.broadcasted_iota(I32, shape, 0)


def lane_of(shape=(8, LANES)):
    return lax.broadcasted_iota(I32, shape, 1)


def run_all(copies):
    for copy in copies:
        copy.start()
    for copy in copies:
        copy.wait()


def repeat(count, step, body):
    def several(n, carry):
        for i in range(step):
            body(n * step + i)
        return carry

    lax.fori_loop(0, count // step, several, 0)


def across(x, row):
    return jnp.broadcast_to(x[row : row + 1, :], (8, LANES))


def product3(left, right, dims):
    (lh, ll), (rh, rl) = left, right
    dot = lambda a, b: lax.dot_general(a, b, (dims, ((), ())), preferred_element_type=F32)
    return dot(lh, rh) + (dot(lh, rl) + dot(ll, rh))


def table_kernel(
    low_hbm, high_hbm, sources_hbm, operators_hbm, keep, give, low, high, sources, operators, sem
):
    half = lax.axis_index("box")
    run_all(
        [
            pltpu.make_async_copy(low_hbm, low, sem.at[0]),
            pltpu.make_async_copy(high_hbm, high, sem.at[1]),
            pltpu.make_async_copy(sources_hbm, sources, sem.at[2]),
            pltpu.make_async_copy(operators_hbm, operators, sem.at[3]),
        ]
    )
    for out, b in ((keep, half), (give, 1 - half)):
        for op in range(20):
            for jh in range(2):
                lanes = pl.ds(pl.multiple_of((2 * b + jh) * LANES, LANES), LANES)
                at = 4 * op + 2 * jh
                out[at : at + 2, :] = high[op, :, lanes]
            out[80 + 2 * op : 82 + 2 * op, :] = low[op]
    give[ROWS:, :] = jnp.zeros((16, LANES), F32)
    give[ROWS:, 0:16] = sources[...].astype(F32)
    give[ROWS:, 16:32] = operators[...].astype(F32)


def ready_kernel(
    rad_hbm, index, weight, angle,
    win_out, wh_out, wl_out, mh_out, ml_out, ci_out, si_out, cx_out, sx_out,
    rad, rows, win, idx, wgt, ang, wh, wl, mh, ml, ci, si, cx, sx, sem, out_sem,
):
    seg, half = lax.axis_index("samp"), lax.axis_index("box")
    start = pl.multiple_of(seg * 512, LANES)
    total = index.shape[1]
    before = pl.multiple_of(jnp.maximum(start - LANES, 0), LANES)
    after = pl.multiple_of(jnp.minimum(start + 512, total - LANES), LANES)
    first = pltpu.make_async_copy(rad_hbm, rad, sem.at[9])
    first.start()
    copies = []
    for n, (src, dst) in enumerate(((index, idx), (weight, wgt), (angle, ang))):
        for m, (at, to, width) in enumerate(((before, 0, 128), (start, 128, 512), (after, 640, 128))):
            copies.append(
                pltpu.make_async_copy(
                    src.at[:, pl.ds(at, width)], dst.at[:, to : to + width], sem.at[3 * n + m]
                )
            )
    for copy in copies:
        copy.start()
    first.wait()
    for c in range(2):
        for o in range(4):
            for r in range(2):
                row = c * 8 + (o // 2) * 4 + r * 2 + o % 2
                rows[row : row + 1, :] = rad[o, r, c : c + 1, :]
    n_samp = rows.shape[1] // LANES
    lane = lane_of((16, LANES))
    lane8 = lane_of()
    block = lambda s: rows[:, (s % n_samp) * LANES : (s % n_samp + 1) * LANES]
    for s in range(n_samp):
        here = block(s)
        real, imag = here[:8], pltpu.roll(here[8:], 64, 1)
        for b, near, low, rest in ((0, s - 1, 0, 96), (1, s + 1, 32, 128)):
            inside = (lane >= low) & (lane < rest)
            inside8 = (lane8 >= low) & (lane8 < rest)
            win[b * n_samp + s, :16, :] = jnp.where(inside, here, block(near))
            win[b * n_samp + s, 16:, :] = jnp.where(inside8, imag, real)
    last = [pltpu.make_async_copy(win, win_out, out_sem.at[0])]
    last[0].start()
    for copy in copies:
        copy.wait()
    slot = lax.broadcasted_iota(I32, (LANES, LANES), 0)

    def band(at, first):
        at = pl.multiple_of(at, LANES)
        found = idx[:, pl.ds(at, LANES)]
        found = found & 127 if first is None else found - first
        value = wgt[:, pl.ds(at, LANES)]
        matrix = jnp.zeros((LANES, LANES), F32)
        for p in range(16):
            matrix += jnp.where(found[p : p + 1, :] == slot, value[p : p + 1, :], 0.0)
        return halves(matrix)

    own = pl.multiple_of(LANES + 256 * half, LANES)

    def interp(n):
        at = pl.multiple_of(n * LANES, LANES)
        wh[:, pl.ds(at, LANES)], wl[:, pl.ds(at, LANES)] = band(own + at, None)

    def anterp(n):
        at = pl.multiple_of(n * LANES, LANES)
        mh[:, pl.ds(at, LANES)], ml[:, pl.ds(at, LANES)] = band(at, seg * 128)

    repeat(2, 2, interp)
    repeat(6, 2, anterp)
    cosine, sine = jnp.cos(ang[...]), jnp.sin(ang[...])
    spin = jnp.where(row_of((4, 768)) % 2 == 0, 1.0, -1.0)
    cx[...] = jnp.concatenate([jnp.broadcast_to(cosine[o : o + 1], (4, 768)) for o in range(8)], 0)
    sx[...] = jnp.concatenate(
        [jnp.broadcast_to(sine[o : o + 1], (4, 768)) * spin for o in range(8)], 0
    )
    for out, x in ((ci, cosine), (si, sine)):
        ang[...] = x
        mine = ang[:, pl.ds(own, 256)]
        for h in range(2):
            pair = [mine[4 * h + 2 * q : 4 * h + 2 * q + 2] for q in range(2)]
            out[h] = jnp.concatenate([pair[0], pair[0], pair[1], pair[1]], 0)
    made = ((wh, wh_out), (wl, wl_out), (mh, mh_out), (ml, ml_out))
    made += ((ci, ci_out), (si, si_out), (cx, cx_out), (sx, sx_out))
    for n, (src, dst) in enumerate(made):
        last.append(pltpu.make_async_copy(src, dst, out_sem.at[n + 1]))
        last[-1].start()
    for copy in last:
        copy.wait()


def upper_kernel(
    tab, got, sources, operators, win, wh_in, wl_in, ci_in, si_in,
    own, oth, rim_own, rim_oth,
    tre, tim, full, pat, pat_sw, wh, wl, ci, si, lists, scalars, sem,
):
    copies = [
        pltpu.make_async_copy(src, dst, sem.at[n])
        for n, (src, dst) in enumerate(((wh_in, wh), (wl_in, wl), (ci_in, ci), (si_in, si)))
    ]
    for copy in copies:
        copy.start()
    lists[:16, 0:16] = sources[...] * 8
    lists[:16, 16:32] = operators[...] * 8
    lists[16:, :] = (got[ROWS:, :] * 8.0).astype(I32)
    listed = pltpu.make_async_copy(lists, scalars, sem.at[4])
    listed.start()
    row = row_of()
    upper, even = row < 4, row % 2 == 0
    flip = jnp.where(even, -1.0, 1.0)
    half = lax.axis_index("box")

    def device(n):
        q = n % 2
        first = (lax.bitwise_xor(q, half) * 8 + n // 2) * 160
        for i in range(20):
            four = tab[n // 2, q, 4 * i : 4 * i + 4, :]
            at = pl.multiple_of(first + 8 * i, 8)
            tre[pl.ds(at, 8), :] = jnp.where(upper, across(four, 0), across(four, 2))
            tim[pl.ds(at, 8), :] = jnp.where(upper, across(four, 1), across(four, 3)) * flip

    repeat(16, 2, device)
    for copy in copies:
        copy.wait()

    def interpolate(n):
        at = pl.multiple_of(n * 128, 128)
        rows = jnp.concatenate([win[n * 8 + q, :16, :] for q in range(8)], 0)
        full[pl.ds(at, 128), :] = product3(
            halves(rows), (wh[...], wl[...]), ((1,), (0,))
        )

    repeat(8, 4, interpolate)

    def aggregate(n):
        u = n
        at = pl.multiple_of(u * 32, 32)
        er, ei, gr, gi = (full[pl.ds(at + 8 * q, 8), :] for q in range(4))
        c0, s0, c1, s1 = ci[0], si[0], ci[1], si[1]
        real = c0 * er - s0 * ei + (c1 * gr - s1 * gi)
        imag = c0 * ei + s0 * er + (c1 * gi + s1 * gr)
        lay, lay_sw = [], []
        for h in range(2):
            re, im = real[:, h * LANES : (h + 1) * LANES], imag[:, h * LANES : (h + 1) * LANES]
            re, im = re + pltpu.roll(re, 4, 0), im + pltpu.roll(im, 4, 0)
            re, im = re + pltpu.roll(re, 7, 0), im + pltpu.roll(im, 7, 0)
            lay.append(jnp.where(even, re, pltpu.roll(im, 1, 0)))
            lay_sw.append(jnp.where(even, im, pltpu.roll(re, 1, 0)))
        to = pl.ds(pl.multiple_of(u * 8, 8), 8)
        pat[to, :] = jnp.where(upper, lay[0], lay[1])
        pat_sw[to, :] = jnp.where(upper, lay_sw[0], lay_sw[1])

    repeat(32, 4, aggregate)

    listed.wait()

    def target(u):
        acc = jnp.zeros((8, LANES), F32)
        acc2 = jnp.zeros((8, LANES), F32)
        for e in range(16):
            src = pl.ds(pl.multiple_of(scalars[u, e], 8), 8)
            op = pl.ds(pl.multiple_of(scalars[u, 16 + e], 8), 8)
            acc += tre[op, :] * pat[src, :]
            acc2 += tim[op, :] * pat_sw[src, :]
        return acc + acc2

    def translate(shift, whole, rim):
        def pair(n):
            one, two = target(2 * n + shift), target(2 * n + 1 + shift)
            whole[2 * n], whole[2 * n + 1] = one, two
            first = jnp.where(upper, one, pltpu.roll(two, 4, 0))
            last = jnp.where(upper, pltpu.roll(one, 4, 0), two)
            rim[n] = jnp.where(half == 0, first, last)

        repeat(8, 2, pair)

    translate(0, own, rim_own)
    translate(16, oth, rim_oth)


def lower_kernel(sources, operators, win, tab, out, t8, pat, lists, scalars, sem):
    lists[:16, :] = sources[...] * 8
    lists[16:, :] = operators[...] * 8
    listed = pltpu.make_async_copy(lists, scalars, sem)
    listed.start()
    row, lane = row_of(), lane_of()
    half = lax.axis_index("box")
    upper, lane_half = row < 4, half * 96
    flip = jnp.where(row % 2 == 0, -1.0, 1.0)

    def device(n):
        q = n % 2
        first = (lax.bitwise_xor(q, half) * 8 + n // 2) * 160
        for i in range(20):
            two = tab[n // 2, q, 80 + 2 * i : 82 + 2 * i, :]
            at = pl.multiple_of(first + 8 * i, 8)
            t8[pl.ds(at, 8), :] = jnp.where(upper, across(two, 0), across(two, 1) * flip)

    repeat(16, 2, device)
    absent = (lane >= 96 - lane_half) & (lane < 128 - lane_half)
    kinds = [(row == 0) | (row == 2), (row == 1) | (row == 3), (row == 4) | (row == 6)]

    def spread_out(n):
        extra = win[n, 16:24, :]
        real = jnp.where(absent, extra, win[n, 0:8, :])
        imag = jnp.where(absent, pltpu.roll(extra, 64, 1), win[n, 8:16, :])
        real_t, imag_t = pltpu.roll(real, 4, 0), pltpu.roll(imag, 4, 0)
        for o2 in range(2):
            if o2 == 0:
                re, im = jnp.where(upper, real, real_t), jnp.where(upper, imag, imag_t)
            else:
                re, im = jnp.where(upper, real_t, real), jnp.where(upper, imag_t, imag)
            later = [re, pltpu.roll(im, 1, 0), im, pltpu.roll(re, 1, 0)]
            sooner = [pltpu.roll(re, 7, 0), im, pltpu.roll(im, 7, 0), re]
            for o, (a, b, c, d) in enumerate((later, sooner)):
                at = pl.multiple_of(n * 32 + 8 * (2 * o2 + o), 8)
                pat[pl.ds(at, 8), :] = jnp.where(
                    kinds[0], a, jnp.where(kinds[1], b, jnp.where(kinds[2], c, d))
                )

    repeat(64, 8, spread_out)
    listed.wait()

    def four(n):
        sums = []
        for q in range(4):
            t = n * 4 + q
            acc = [jnp.zeros((8, LANES), F32)] * 2
            for e in range(16):
                op = pl.ds(pl.multiple_of(scalars[16 + e, t], 8), 8)
                src = pl.ds(pl.multiple_of(scalars[e, t], 8), 8)
                acc[e % 2] += t8[op, :] * pat[src, :]
            total = acc[0] + acc[1]
            sums.append(total + pltpu.roll(total, 4, 0))
        out[2 * n] = jnp.where(upper, sums[0], sums[1])
        out[2 * n + 1] = jnp.where(upper, sums[2], sums[3])

    repeat(32, 1, four)


def final_kernel(
    own, got, rim_a, rim_b, low, mh, ml, cx, sx, low_out, high_out, lh, ll
):
    row = row_of()
    upper, even = row < 4, row % 2 == 0
    first = lax.axis_index("box") == 0

    def swap(x):
        return jnp.where(even, pltpu.roll(x, 7, 0), pltpu.roll(x, 1, 0))

    def pair(n):
        rims = (jnp.where(first, rim_b[n], rim_a[n]), jnp.where(first, rim_a[n], rim_b[n]))
        for q in range(2):
            u = 2 * n + q
            one = jnp.where(first, own[u], got[u])
            two = jnp.where(first, got[u], own[u])
            for jt, x in enumerate((one, one, two, two)):
                for r in range(2):
                    high_out[u, r, :, jt * LANES : (jt + 1) * LANES] = x[
                        4 * (jt % 2) + 2 * r : 4 * (jt % 2) + 2 * r + 2, :
                    ]
            blocks = []
            for x in (one, two):
                turned = pltpu.roll(x, 4, 0)
                blocks += [jnp.where(upper, x, turned), jnp.where(upper, turned, x)]
            edge = []
            for x in rims:
                turned = pltpu.roll(x, 4, 0)
                edge.append(jnp.where(upper, x, turned) if q == 0 else jnp.where(upper, turned, x))
            blocks = [edge[0]] + blocks + [edge[1]]
            at = pl.multiple_of(u * 32, 32)
            for jt, x in enumerate(blocks):
                lanes = slice(jt * LANES, (jt + 1) * LANES)
                y = swap(x)
                rows = jnp.concatenate(
                    [
                        cx[8 * g : 8 * g + 8, lanes] * x + sx[8 * g : 8 * g + 8, lanes] * y
                        for g in range(4)
                    ],
                    0,
                )
                lh[pl.ds(at, 32), lanes], ll[pl.ds(at, 32), lanes] = halves(rows)

    repeat(8, 2, pair)

    def block(n):
        at = pl.multiple_of(n * 128, 128)
        sums = product3(
            (lh[pl.ds(at, 128), :], ll[pl.ds(at, 128), :]), (mh[...], ml[...]), ((1,), (1,))
        )
        low_out[pl.ds(at, 128), :] = sums + low[pl.ds(at, 128), :]

    repeat(4, 2, block)


def shards(
    radiated,
    low_table,
    high_table,
    low_sources,
    low_operators,
    high_sources,
    high_operators,
    stencil_index,
    stencil_weight,
    shift_angle,
):
    n_samp = lax.axis_size("samp")
    dma = pltpu.SemaphoreType.DMA
    keep, give = call(
        table_kernel,
        [HBM] * 4,
        [((ROWS, LANES), F32), ((SENT, LANES), F32)],
        [pltpu.VMEM((20, 2, LANES), F32), pltpu.VMEM((20, 2, 512), F32)]
        + [pltpu.VMEM((16, 16), I32)] * 2
        + [dma((4,))],
        moved=1 << 20,
        room=ALL_VMEM,
    )(low_table, high_table, high_sources, high_operators)
    got = lax.ppermute(give, "box", [(0, 1), (1, 0)])
    made = [
        ((64, 24, LANES), F32),
        ((LANES, 256), BF16),
        ((LANES, 256), BF16),
        ((LANES, 768), BF16),
        ((LANES, 768), BF16),
        ((2, 8, 256), F32),
        ((2, 8, 256), F32),
        ((32, 768), F32),
        ((32, 768), F32),
    ]
    win, wh, wl, mh, ml, ci, si, cx, sx = call(
        ready_kernel,
        [HBM] * 4,
        made,
        [pltpu.VMEM((4, 2, 2, 4096), F32), pltpu.VMEM((16, 4096), F32), pltpu.VMEM(*made[0])]
        + [pltpu.VMEM((16, 768), I32), pltpu.VMEM((16, 768), F32), pltpu.VMEM((8, 768), F32)]
        + [pltpu.VMEM(*x) for x in made[1:]]
        + [dma((10,)), dma((9,))],
        flops=10 << 20,
        moved=8 << 20,
        out_place=HBM,
        room=ALL_VMEM,
    )(radiated, stencil_index, stencil_weight, shift_angle)
    win, got = lax.optimization_barrier((win, got))
    win = lax.all_to_all(win, ("box", "samp"), 0, 0, tiled=True)
    tab = lax.all_gather(jnp.stack([keep, got[:ROWS]]), "rhs")
    part, rim = ((16, 8, LANES), F32), ((8, 8, LANES), F32)
    own, oth, rim_own, rim_oth = call(
        upper_kernel,
        [VMEM] * 5 + [HBM] * 4,
        [part, part, rim, rim],
        [
            pltpu.VMEM((2560, LANES), F32),
            pltpu.VMEM((2560, LANES), F32),
            pltpu.VMEM((1024, 256), F32),
            pltpu.VMEM((256, LANES), F32),
            pltpu.VMEM((256, LANES), F32),
            pltpu.VMEM(*made[1]),
            pltpu.VMEM(*made[2]),
            pltpu.VMEM(*made[5]),
            pltpu.VMEM(*made[6]),
            pltpu.VMEM((32, LANES), I32),
            pltpu.SMEM((32, LANES), I32),
            dma((5,)),
        ],
        flops=200 << 20,
        moved=6 << 20,
    )(tab, got, high_sources, high_operators, win, wh, wl, ci, si)
    flat = lambda s, b: 2 * s + b
    other = lax.ppermute(oth, "box", [(0, 1), (1, 0)])
    down = [(flat(s, 0), s - 1) for s in range(1, n_samp)]
    up = [(flat(s, 1), s + 1) for s in range(n_samp - 1)]
    both = ("samp", "box")
    rim_a = lax.ppermute(
        rim_own, both, [(i, flat(s, 0)) for i, s in down] + [(i, flat(s, 1)) for i, s in up]
    )
    rim_b = lax.ppermute(
        rim_oth, both, [(i, flat(s, 1)) for i, s in down] + [(i, flat(s, 0)) for i, s in up]
    )
    (low,) = call(
        lower_kernel,
        [VMEM] * 4,
        [((64, 8, LANES), F32)],
        [
            pltpu.VMEM((2560, LANES), F32),
            pltpu.VMEM((2048, LANES), F32),
            pltpu.VMEM((32, LANES), I32),
            pltpu.SMEM((32, LANES), I32),
            dma,
        ],
        flops=20 << 20,
        moved=10 << 20,
    )(low_sources.T, low_operators.T, win, tab)
    low_incoming, high_incoming = call(
        final_kernel,
        [VMEM] * 9,
        [((512, LANES), F32), ((16, 2, 2, 512), F32)],
        [pltpu.VMEM((512, 768), BF16), pltpu.VMEM((512, 768), BF16)],
        flops=300 << 20,
        moved=4 << 20,
    )(own, other, rim_a, rim_b, low.reshape(512, LANES), mh, ml, cx, sx)
    return low_incoming.reshape(128, 2, 2, LANES), high_incoming


def solution(mesh):
    return jax.shard_map(
        shards,
        mesh=mesh,
        in_specs=(
            P(("box", "samp"), "rhs", None, None),
            P(("box", "rhs"), None, "samp"),
            P(("box", "rhs"), None, "samp"),
            P("box", None),
            P("box", None),
            P("box", None),
            P("box", None),
            P(),
            P(),
            P(),
        ),
        out_specs=(P("box", "rhs", None, "samp"), P("box", "rhs", None, "samp")),
        check_vma=False,
    )
```

```python
import jax
import jax.numpy as jnp
from jax import lax
from jax.experimental import pallas as pl
from jax.experimental.pallas import tpu as pltpu
from jax.sharding import PartitionSpec as P

F32, BF16, I32 = jnp.float32, jnp.bfloat16, jnp.int32
VMEM = pl.BlockSpec(memory_space=pltpu.VMEM)
SMEM = pl.BlockSpec(memory_space=pltpu.SMEM)
HBM = pl.BlockSpec(memory_space=pltpu.HBM)
LANES = 128
ROWS = 120
ALL_VMEM = 63 << 20
SENT = ROWS + 16


def call(kernel, ins, outs, scratch=(), flops=0, moved=0, out_place=VMEM, room=24 << 20):
    return pl.pallas_call(
        kernel,
        in_specs=list(ins),
        out_specs=[out_place] * len(outs),
        out_shape=[jax.ShapeDtypeStruct(s, d) for s, d in outs],
        scratch_shapes=list(scratch),
        compiler_params=pltpu.CompilerParams(vmem_limit_bytes=room),
        cost_estimate=pl.CostEstimate(flops=flops, bytes_accessed=moved, transcendentals=0),
    )


def halves(x):
    high = x.astype(BF16)
    return high, (x - high.astype(F32)).astype(BF16)


def row_of(shape=(8, LANES)):
    return lax.broadcasted_iota(I32, shape, 0)


def lane_of(shape=(8, LANES)):
    return lax.broadcasted_iota(I32, shape, 1)


def run_all(copies):
    for copy in copies:
        copy.start()
    for copy in copies:
        copy.wait()


def repeat(count, step, body):
    def several(n, carry):
        for i in range(step):
            body(n * step + i)
        return carry

    lax.fori_loop(0, count // step, several, 0)


def swap(x):
    return jnp.where(row_of() % 2 == 0, pltpu.roll(x, 7, 0), pltpu.roll(x, 1, 0))


def across(x, row):
    return jnp.broadcast_to(x[row : row + 1, :], (8, LANES))


def product3(left, right, dims):
    (lh, ll), (rh, rl) = left, right
    dot = lambda a, b: lax.dot_general(a, b, (dims, ((), ())), preferred_element_type=F32)
    return dot(lh, rh) + (dot(lh, rl) + dot(ll, rh))


def block_of(n):
    return (lax.bitwise_xor(n % 2, lax.axis_index("box")) * 8 + n // 2) * 160


def table_kernel(
    low_hbm, high_hbm, sources_hbm, operators_hbm, pair, give, low, high, sources, operators, sem
):
    half = lax.axis_index("box")
    run_all(
        [
            pltpu.make_async_copy(low_hbm, low, sem.at[0]),
            pltpu.make_async_copy(high_hbm, high, sem.at[1]),
            pltpu.make_async_copy(sources_hbm, sources, sem.at[2]),
            pltpu.make_async_copy(operators_hbm, operators, sem.at[3]),
        ]
    )
    for out, b in ((give, 1 - half), (pair.at[0], half)):
        for op in range(20):
            for jh in range(2):
                lanes = pl.ds(pl.multiple_of((2 * b + jh) * LANES, LANES), LANES)
                at = 4 * op + 2 * jh
                out[at : at + 2, :] = high[op, :, lanes]
            out[80 + 2 * op : 82 + 2 * op, :] = low[op]
    give[ROWS:, :] = jnp.zeros((16, LANES), F32)
    give[ROWS:, 0:16] = sources[...].astype(F32)
    give[ROWS:, 16:32] = operators[...].astype(F32)


def ready_kernel(
    rad_hbm, index, weight, angle, sources_hbm, operators_hbm,
    win_out, w_out, m_out, spin_out,
    rad, rows, win, idx, wgt, ang, w, m, spins, sources, operators, sem, out_sem,
):
    seg, half = lax.axis_index("samp"), lax.axis_index("box")
    start = pl.multiple_of(seg * 512, LANES)
    total = index.shape[1]
    before = pl.multiple_of(jnp.maximum(start - LANES, 0), LANES)
    after = pl.multiple_of(jnp.minimum(start + 512, total - LANES), LANES)
    first = pltpu.make_async_copy(rad_hbm, rad, sem.at[9])
    first.start()
    copies = []
    for n, (src, dst) in enumerate(((index, idx), (weight, wgt), (angle, ang))):
        for k, (at, to, width) in enumerate(((before, 0, 128), (start, 128, 512), (after, 640, 128))):
            copies.append(
                pltpu.make_async_copy(
                    src.at[:, pl.ds(at, width)], dst.at[:, to : to + width], sem.at[3 * n + k]
                )
            )
    copies.append(pltpu.make_async_copy(sources_hbm, sources, sem.at[10]))
    copies.append(pltpu.make_async_copy(operators_hbm, operators, sem.at[11]))
    for copy in copies:
        copy.start()
    first.wait()
    for o in range(4):
        for r in range(2):
            rows[4 * o + 2 * r : 4 * o + 2 * r + 2, :] = rad[o, r]
    n_samp = rows.shape[1] // LANES
    lane = lane_of((16, LANES))
    lane8 = lane_of()
    block = lambda s: rows[:, (s % n_samp) * LANES : (s % n_samp + 1) * LANES]
    for s in range(n_samp):
        here = block(s)
        near_rows, far_rows = here[:8], pltpu.roll(here[8:], 64, 1)
        for b, near, low, rest in ((0, s - 1, 0, 96), (1, s + 1, 32, 128)):
            inside = (lane >= low) & (lane < rest)
            inside8 = (lane8 >= low) & (lane8 < rest)
            win[b * n_samp + s, :16, :] = jnp.where(inside, here, block(near))
            win[b * n_samp + s, 16:, :] = jnp.where(inside8, far_rows, near_rows)
    last = [pltpu.make_async_copy(win, win_out, out_sem.at[0])]
    last[0].start()
    for copy in copies:
        copy.wait()
    slot = lax.broadcasted_iota(I32, (LANES, LANES), 0)

    def band(at, first):
        at = pl.multiple_of(at, LANES)
        found = idx[:, pl.ds(at, LANES)]
        found = found & 127 if first is None else found - first
        value = wgt[:, pl.ds(at, LANES)]
        matrix = jnp.zeros((LANES, LANES), F32)
        for p in range(16):
            matrix += jnp.where(found[p : p + 1, :] == slot, value[p : p + 1, :], 0.0)
        return halves(matrix)

    own = pl.multiple_of(LANES + 256 * half, LANES)

    def interp(n):
        at = pl.multiple_of(n * LANES, LANES)
        w[:LANES, pl.ds(at, LANES)], w[LANES:, pl.ds(at, LANES)] = band(own + at, None)

    def anterp(n):
        at = pl.multiple_of(n * LANES, LANES)
        m[:LANES, pl.ds(at, LANES)], m[LANES:, pl.ds(at, LANES)] = band(at, seg * 128)

    cosine, sine = jnp.cos(ang[...]), jnp.sin(ang[...])
    spin = jnp.where(row_of((4, 768)) % 2 == 0, 1.0, -1.0)
    spins[:32, :] = jnp.concatenate(
        [jnp.broadcast_to(cosine[o : o + 1], (4, 768)) for o in range(8)], 0
    )
    spins[32:64, :] = jnp.concatenate(
        [jnp.broadcast_to(sine[o : o + 1], (4, 768)) * spin for o in range(8)], 0
    )
    spins[64:, :] = jnp.zeros((16, 768), F32)
    spins[64:, 0:16] = sources[...].astype(F32)
    spins[64:, 16:32] = operators[...].astype(F32)

    def send(src, dst):
        last.append(pltpu.make_async_copy(src, dst, out_sem.at[len(last)]))
        last[-1].start()

    send(spins, spin_out)
    repeat(2, 2, interp)
    send(w, w_out)
    repeat(6, 2, anterp)
    send(m, m_out)
    for copy in last:
        copy.wait()


def upper_kernel(
    tab, got, win, w_in, spin_in,
    own, oth, rim_own, rim_oth,
    tre, tim, full, pat, same, cross, w, spins, lists, scalars, sem,
):
    half = lax.axis_index("box")
    lanes = pl.ds(pl.multiple_of(LANES + 256 * half, LANES), 256)
    copies = [
        pltpu.make_async_copy(spin_in.at[pl.ds(64, 16), pl.ds(0, LANES)], spins.at[64:, 0:LANES], sem.at[0]),
        pltpu.make_async_copy(w_in, w, sem.at[1]),
        pltpu.make_async_copy(spin_in.at[pl.ds(0, 64), lanes], spins.at[0:64, :], sem.at[2]),
    ]
    for copy in copies:
        copy.start()
    lists[16:, :] = (got[ROWS:, :] * 8.0).astype(I32)
    copies[0].wait()
    lists[:16, :] = (spins[64:, :LANES] * 8.0).astype(I32)
    listed = pltpu.make_async_copy(lists, scalars, sem.at[3])
    listed.start()
    row = row_of()
    upper = row < 4
    flip = jnp.where(row % 2 == 0, 1.0, -1.0)

    def device(n):
        first = block_of(n)
        for i in range(20):
            four = tab[n, 4 * i : 4 * i + 4, :]
            at = pl.multiple_of(first + 8 * i, 8)
            tre[pl.ds(at, 8), :] = jnp.where(upper, across(four, 0), across(four, 2))
            tim[pl.ds(at, 8), :] = jnp.where(upper, across(four, 1), across(four, 3)) * flip

    repeat(16, 2, device)
    copies[1].wait()

    def interpolate(n):
        at = pl.multiple_of(n * 128, 128)
        rows = jnp.concatenate([win[n * 8 + q, :16, :] for q in range(8)], 0)
        full[pl.ds(at, 128), :] = product3(halves(rows), (w[:LANES], w[LANES:]), ((1,), (0,)))

    repeat(8, 4, interpolate)
    copies[2].wait()

    def aggregate(u):
        at = pl.multiple_of(u * 32, 32)
        lay = []
        for h in range(2):
            lanes = slice(h * LANES, (h + 1) * LANES)
            straight = turned = 0.0
            for k in range(4):
                x = full[pl.ds(at + 8 * k, 8), lanes]
                straight += spins[8 * k : 8 * k + 8, lanes] * x
                turned += spins[32 + 8 * k : 40 + 8 * k, lanes] * x
            total = straight + swap(turned)
            lay.append(total + pltpu.roll(total, 4, 0))
        pat[pl.ds(pl.multiple_of(u * 8, 8), 8), :] = jnp.where(upper, lay[0], lay[1])

    repeat(32, 4, aggregate)
    listed.wait()

    def translate(n):
        for q in range(2):
            u = 2 * n + q
            acc = jnp.zeros((8, LANES), F32)
            acc2 = jnp.zeros((8, LANES), F32)
            for e in range(16):
                x = pat[pl.ds(pl.multiple_of(scalars[u, e], 8), 8), :]
                op = pl.ds(pl.multiple_of(scalars[u, 16 + e], 8), 8)
                acc += tre[op, :] * x
                acc2 += tim[op, :] * x
            same[u], cross[u] = acc, acc2

    repeat(16, 2, translate)

    def border(n):
        for whole, rim, shift in ((own, rim_own, 0), (oth, rim_oth, 16)):
            one = same[2 * n + shift] + swap(cross[2 * n + shift])
            two = same[2 * n + 1 + shift] + swap(cross[2 * n + 1 + shift])
            whole[2 * n], whole[2 * n + 1] = one, two
            first = jnp.where(upper, one, pltpu.roll(two, 4, 0))
            last = jnp.where(upper, pltpu.roll(one, 4, 0), two)
            rim[n] = jnp.where(half == 0, first, last)

    repeat(8, 8, border)


def lower_kernel(sources, operators, win, tab, out, t8, pat, full, lists, scalars, sem):
    by_target = [jnp.transpose(x[...] * 8) for x in (sources, operators)]
    for q in range(4):
        for k in range(2):
            lists[:, 32 * q + 16 * k : 32 * q + 16 * k + 16] = by_target[k][32 * q : 32 * q + 32]
    listed = pltpu.make_async_copy(lists, scalars, sem)
    listed.start()
    row, lane = row_of(), lane_of()
    upper, lane_half = row < 4, lax.axis_index("box") * 96
    flip = jnp.where(upper | (row % 2 == 0), 1.0, -1.0)
    absent = (lane >= 96 - lane_half) & (lane < 128 - lane_half)

    def device(n):
        first = block_of(n)
        for i in range(20):
            two = tab[n, 80 + 2 * i : 82 + 2 * i, :]
            at = pl.multiple_of(first + 8 * i, 8)
            t8[pl.ds(at, 8), :] = jnp.where(upper, across(two, 0), across(two, 1)) * flip

    repeat(16, 2, device)
    def spread_out(n):
        extra = win[n, 16:24, :]
        for v, x in enumerate((extra, pltpu.roll(extra, 64, 1))):
            x = jnp.where(absent, x, win[n, 8 * v : 8 * v + 8, :])
            turned = pltpu.roll(x, 4, 0)
            at = pl.multiple_of(n * 32 + 16 * v, 8)
            pat[pl.ds(at, 8), :] = jnp.where(upper, x, turned)
            pat[pl.ds(at + 8, 8), :] = jnp.where(upper, turned, x)

    repeat(64, 8, spread_out)
    listed.wait()

    def four(n):
        for q in range(4):
            acc = [jnp.zeros((8, LANES), F32)] * 2
            for e in range(16):
                op = pl.ds(pl.multiple_of(scalars[n, 32 * q + 16 + e], 8), 8)
                src = pl.ds(pl.multiple_of(scalars[n, 32 * q + e], 8), 8)
                acc[e % 2] += t8[op, :] * pat[src, :]
            full[32 * q + n] = acc[0] + acc[1]

    repeat(32, 1, four)

    def fold(n):
        one, two = full[2 * n], full[2 * n + 1]
        same = jnp.where(upper, one, pltpu.roll(two, 4, 0))
        out[n] = same + swap(jnp.where(upper, pltpu.roll(one, 4, 0), two))

    repeat(64, 16, fold)


def final_kernel(
    own, got, rim_a, rim_b, low, m, spins, low_out, high_out, lh, ll
):
    row = row_of()
    upper = row < 4
    first = lax.axis_index("box") == 0

    def pair(n):
        rims = (jnp.where(first, rim_b[n], rim_a[n]), jnp.where(first, rim_a[n], rim_b[n]))
        for q in range(2):
            u = 2 * n + q
            one = jnp.where(first, own[u], got[u])
            two = jnp.where(first, got[u], own[u])
            for jt, x in enumerate((one, one, two, two)):
                for r in range(2):
                    high_out[u, r, :, jt * LANES : (jt + 1) * LANES] = x[
                        4 * (jt % 2) + 2 * r : 4 * (jt % 2) + 2 * r + 2, :
                    ]
            blocks = []
            for x in (one, two):
                turned = pltpu.roll(x, 4, 0)
                blocks += [jnp.where(upper, x, turned), jnp.where(upper, turned, x)]
            edge = []
            for x in rims:
                turned = pltpu.roll(x, 4, 0)
                edge.append(jnp.where(upper, x, turned) if q == 0 else jnp.where(upper, turned, x))
            blocks = [edge[0]] + blocks + [edge[1]]
            at = pl.multiple_of(u * 32, 32)
            for jt, x in enumerate(blocks):
                lanes = slice(jt * LANES, (jt + 1) * LANES)
                y = swap(x)
                rows = jnp.concatenate(
                    [
                        spins[8 * g : 8 * g + 8, lanes] * x + spins[32 + 8 * g : 40 + 8 * g, lanes] * y
                        for g in range(4)
                    ],
                    0,
                )
                lh[pl.ds(at, 32), lanes], ll[pl.ds(at, 32), lanes] = halves(rows)

    repeat(8, 2, pair)

    def block(n):
        at = pl.multiple_of(n * 128, 128)
        sums = product3(
            (lh[pl.ds(at, 128), :], ll[pl.ds(at, 128), :]), (m[:LANES, :], m[LANES:, :]), ((1,), (1,))
        )
        low_out[pl.ds(at, 128), :] = sums + low[pl.ds(at, 128), :]

    repeat(4, 2, block)


def shards(
    radiated,
    low_table,
    high_table,
    low_sources,
    low_operators,
    high_sources,
    high_operators,
    stencil_index,
    stencil_weight,
    shift_angle,
):
    n_samp = lax.axis_size("samp")
    dma = pltpu.SemaphoreType.DMA
    pair, give = call(
        table_kernel,
        [HBM] * 4,
        [((2, ROWS, LANES), F32), ((SENT, LANES), F32)],
        [pltpu.VMEM((20, 2, LANES), F32), pltpu.VMEM((20, 2, 512), F32)]
        + [pltpu.VMEM((16, 16), I32)] * 2
        + [dma((4,))],
        moved=1 << 20,
        room=ALL_VMEM,
    )(low_table, high_table, high_sources, high_operators)
    got = lax.ppermute(give, "box", [(0, 1), (1, 0)])
    made = [
        ((64, 24, LANES), F32),
        ((256, 256), BF16),
        ((256, 768), BF16),
        ((80, 768), F32),
    ]
    win, w, m, spins = call(
        ready_kernel,
        [HBM] * 6,
        made,
        [pltpu.VMEM((4, 2, 2, 4096), F32), pltpu.VMEM((16, 4096), F32), pltpu.VMEM(*made[0])]
        + [pltpu.VMEM((16, 768), I32), pltpu.VMEM((16, 768), F32), pltpu.VMEM((8, 768), F32)]
        + [pltpu.VMEM(*x) for x in made[1:]]
        + [pltpu.VMEM((16, 16), I32)] * 2
        + [dma((12,)), dma((4,))],
        flops=10 << 20,
        moved=8 << 20,
        out_place=HBM,
        room=ALL_VMEM,
    )(radiated, stencil_index, stencil_weight, shift_angle, high_sources, high_operators)
    win, got = lax.optimization_barrier((win, got))
    win = lax.all_to_all(win, ("box", "samp"), 0, 0, tiled=True)
    tab = lax.all_gather(pair.at[1].set(got[:ROWS]), "rhs", tiled=True)
    part, rim = ((16, 8, LANES), F32), ((8, 8, LANES), F32)
    own, oth, rim_own, rim_oth = call(
        upper_kernel,
        [VMEM] * 3 + [HBM] * 2,
        [part, part, rim, rim],
        [
            pltpu.VMEM((2560, LANES), F32),
            pltpu.VMEM((2560, LANES), F32),
            pltpu.VMEM((1024, 256), F32),
            pltpu.VMEM((256, LANES), F32),
            pltpu.VMEM((32, 8, LANES), F32),
            pltpu.VMEM((32, 8, LANES), F32),
            pltpu.VMEM(*made[1]),
            pltpu.VMEM((80, 256), F32),
            pltpu.VMEM((32, LANES), I32),
            pltpu.SMEM((32, LANES), I32),
            dma((4,)),
        ],
        flops=200 << 20,
        moved=6 << 20,
    )(tab, got, win, w, spins)
    flat = lambda s, b: 2 * s + b
    other = lax.ppermute(oth, "box", [(0, 1), (1, 0)])
    down = [(flat(s, 0), s - 1) for s in range(1, n_samp)]
    up = [(flat(s, 1), s + 1) for s in range(n_samp - 1)]
    both = ("samp", "box")
    rim_a = lax.ppermute(
        rim_own, both, [(i, flat(s, 0)) for i, s in down] + [(i, flat(s, 1)) for i, s in up]
    )
    rim_b = lax.ppermute(
        rim_oth, both, [(i, flat(s, 1)) for i, s in down] + [(i, flat(s, 0)) for i, s in up]
    )
    (low,) = call(
        lower_kernel,
        [VMEM] * 4,
        [((64, 8, LANES), F32)],
        [
            pltpu.VMEM((2560, LANES), F32),
            pltpu.VMEM((2048, LANES), F32),
            pltpu.VMEM((LANES, 8, LANES), F32),
            pltpu.VMEM((32, LANES), I32),
            pltpu.SMEM((32, LANES), I32),
            dma,
        ],
        flops=20 << 20,
        moved=10 << 20,
    )(low_sources.T, low_operators.T, win, tab)
    low_incoming, high_incoming = call(
        final_kernel,
        [VMEM] * 7,
        [((512, LANES), F32), ((16, 2, 2, 512), F32)],
        [pltpu.VMEM((512, 768), BF16), pltpu.VMEM((512, 768), BF16)],
        flops=300 << 20,
        moved=4 << 20,
    )(own, other, rim_a, rim_b, low.reshape(512, LANES), m, spins)
    return low_incoming.reshape(128, 2, 2, LANES), high_incoming


def solution(mesh):
    return jax.shard_map(
        shards,
        mesh=mesh,
        in_specs=(
            P(("box", "samp"), "rhs", None, None),
            P(("box", "rhs"), None, "samp"),
            P(("box", "rhs"), None, "samp"),
            P("box", None),
            P("box", None),
            P("box", None),
            P("box", None),
            P(),
            P(),
            P(),
        ),
        out_specs=(P("box", "rhs", None, "samp"), P("box", "rhs", None, "samp")),
        check_vma=False,
    )
```

```python
import jax
import jax.numpy as jnp
from jax import lax
from jax.experimental import pallas as pl
from jax.experimental.pallas import tpu as pltpu
from jax.sharding import PartitionSpec as P

F32, BF16, I32 = jnp.float32, jnp.bfloat16, jnp.int32
VMEM = pl.BlockSpec(memory_space=pltpu.VMEM)
SMEM = pl.BlockSpec(memory_space=pltpu.SMEM)
HBM = pl.BlockSpec(memory_space=pltpu.HBM)
LANES = 128
ROWS = 120
ALL_VMEM = 63 << 20
SENT = ROWS + 16


def call(kernel, ins, outs, scratch=(), flops=0, moved=0, out_place=VMEM, room=24 << 20):
    return pl.pallas_call(
        kernel,
        in_specs=list(ins),
        out_specs=[out_place] * len(outs),
        out_shape=[jax.ShapeDtypeStruct(s, d) for s, d in outs],
        scratch_shapes=list(scratch),
        compiler_params=pltpu.CompilerParams(vmem_limit_bytes=room),
        cost_estimate=pl.CostEstimate(flops=flops, bytes_accessed=moved, transcendentals=0),
    )


def halves(x):
    high = x.astype(BF16)
    return high, (x - high.astype(F32)).astype(BF16)


def row_of(shape=(8, LANES)):
    return lax.broadcasted_iota(I32, shape, 0)


def lane_of(shape=(8, LANES)):
    return lax.broadcasted_iota(I32, shape, 1)


def run_all(copies):
    for copy in copies:
        copy.start()
    for copy in copies:
        copy.wait()


def repeat(count, step, body):
    def several(n, carry):
        for i in range(step):
            body(n * step + i)
        return carry

    lax.fori_loop(0, count // step, several, 0)


def swap(x):
    return jnp.where(row_of() % 2 == 0, pltpu.roll(x, 7, 0), pltpu.roll(x, 1, 0))


def across(x, row):
    return jnp.broadcast_to(x[row : row + 1, :], (8, LANES))


def product3(left, right, dims):
    (lh, ll), (rh, rl) = left, right
    dot = lambda a, b: lax.dot_general(a, b, (dims, ((), ())), preferred_element_type=F32)
    return dot(lh, rh) + (dot(lh, rl) + dot(ll, rh))


def block_of(n):
    return (lax.bitwise_xor(n % 2, lax.axis_index("box")) * 8 + n // 2) * 160


def pack_tables(low, high, b, out):
    for op in range(20):
        for jh in range(2):
            lanes = pl.ds(pl.multiple_of((2 * b + jh) * LANES, LANES), LANES)
            at = 4 * op + 2 * jh
            out[at : at + 2, :] = high[op, :, lanes]
        out[80 + 2 * op : 82 + 2 * op, :] = low[op]


def table_kernel(
    low_hbm, high_hbm, sources_hbm, operators_hbm, give, low, high, sources, operators, sem
):
    run_all(
        [
            pltpu.make_async_copy(low_hbm, low, sem.at[0]),
            pltpu.make_async_copy(high_hbm, high, sem.at[1]),
            pltpu.make_async_copy(sources_hbm, sources, sem.at[2]),
            pltpu.make_async_copy(operators_hbm, operators, sem.at[3]),
        ]
    )
    pack_tables(low, high, 1 - lax.axis_index("box"), give)
    give[ROWS:, :] = jnp.zeros((16, LANES), F32)
    give[ROWS:, 0:16] = sources[...].astype(F32)
    give[ROWS:, 16:32] = operators[...].astype(F32)


def ready_kernel(
    rad_hbm, index, weight, angle, sources_hbm, operators_hbm, low_hbm, high_hbm,
    win_out, w_out, m_out, spin_out, pair_out,
    rad, rows, win, idx, wgt, ang, w, m, spins, sources, operators, low_own, high_own, keep, sem, out_sem,
):
    seg, half = lax.axis_index("samp"), lax.axis_index("box")
    start = pl.multiple_of(seg * 512, LANES)
    total = index.shape[1]
    before = pl.multiple_of(jnp.maximum(start - LANES, 0), LANES)
    after = pl.multiple_of(jnp.minimum(start + 512, total - LANES), LANES)
    first = pltpu.make_async_copy(rad_hbm, rad, sem.at[9])
    first.start()
    copies = []
    for n, (src, dst) in enumerate(((index, idx), (weight, wgt), (angle, ang))):
        for k, (at, to, width) in enumerate(((before, 0, 128), (start, 128, 512), (after, 640, 128))):
            copies.append(
                pltpu.make_async_copy(
                    src.at[:, pl.ds(at, width)], dst.at[:, to : to + width], sem.at[3 * n + k]
                )
            )
    copies.append(pltpu.make_async_copy(sources_hbm, sources, sem.at[10]))
    copies.append(pltpu.make_async_copy(operators_hbm, operators, sem.at[11]))
    copies.append(pltpu.make_async_copy(low_hbm, low_own, sem.at[12]))
    copies.append(pltpu.make_async_copy(high_hbm, high_own, sem.at[13]))
    for copy in copies:
        copy.start()
    first.wait()
    for o in range(4):
        for r in range(2):
            rows[4 * o + 2 * r : 4 * o + 2 * r + 2, :] = rad[o, r]
    n_samp = rows.shape[1] // LANES
    lane = lane_of((16, LANES))
    lane8 = lane_of()
    block = lambda s: rows[:, (s % n_samp) * LANES : (s % n_samp + 1) * LANES]
    for s in range(n_samp):
        here = block(s)
        near_rows, far_rows = here[:8], pltpu.roll(here[8:], 64, 1)
        for b, near, low, rest in ((0, s - 1, 0, 96), (1, s + 1, 32, 128)):
            inside = (lane >= low) & (lane < rest)
            inside8 = (lane8 >= low) & (lane8 < rest)
            win[b * n_samp + s, :16, :] = jnp.where(inside, here, block(near))
            win[b * n_samp + s, 16:, :] = jnp.where(inside8, far_rows, near_rows)
    last = [pltpu.make_async_copy(win, win_out, out_sem.at[0])]
    last[0].start()
    for copy in copies:
        copy.wait()

    def band(at, first, low=0, rest=LANES):
        found = idx[:, pl.ds(at, LANES)]
        found = found & 127 if first is None else found - first
        value = wgt[:, pl.ds(at, LANES)]
        matrix = jnp.zeros((rest - low, LANES), F32)
        slot = row_of((rest - low, LANES)) + low
        for p in range(16):
            matrix += jnp.where(found[p : p + 1, :] == slot, value[p : p + 1, :], 0.0)
        return halves(matrix)

    own = pl.multiple_of(LANES + 256 * half, LANES)

    cosine, sine = jnp.cos(ang[...]), jnp.sin(ang[...])
    spin = jnp.where(row_of((4, 768)) % 2 == 0, 1.0, -1.0)
    spins[:32, :] = jnp.concatenate(
        [jnp.broadcast_to(cosine[o : o + 1], (4, 768)) for o in range(8)], 0
    )
    spins[32:64, :] = jnp.concatenate(
        [jnp.broadcast_to(sine[o : o + 1], (4, 768)) * spin for o in range(8)], 0
    )
    spins[64:, :] = jnp.zeros((16, 768), F32)
    spins[64:, 0:16] = sources[...].astype(F32)
    spins[64:, 16:32] = operators[...].astype(F32)

    def send(src, dst):
        last.append(pltpu.make_async_copy(src, dst, out_sem.at[len(last)]))
        last[-1].start()

    send(spins, spin_out)
    pack_tables(low_own, high_own, half, keep)
    send(keep, pair_out.at[0])
    for n in range(2):
        lanes = slice(n * LANES, (n + 1) * LANES)
        w[:LANES, lanes], w[LANES:, lanes] = band(
            pl.multiple_of(own + n * LANES, LANES), None
        )
    send(w, w_out)
    m[...] = jnp.zeros_like(m)
    for n in range(6):
        lanes, low, rest = slice(n * LANES, (n + 1) * LANES), max(32 * n - 64, 0), min(32 * n + 32, LANES)
        m[low:rest, lanes], m[LANES + low : LANES + rest, lanes] = band(
            n * LANES, seg * 128, low, rest
        )
    send(m, m_out)
    for copy in last:
        copy.wait()


def upper_kernel(
    tab, got, win, w, spins,
    own, oth, rim_own, rim_oth,
    tre, tim, full, pat, same, cross, lists, scalars, sem,
):
    half = lax.axis_index("box")
    lists[:16, :] = (spins[64:, :LANES] * 8.0).astype(I32)
    lists[16:, :] = (got[ROWS:, :] * 8.0).astype(I32)
    listed = pltpu.make_async_copy(lists, scalars, sem)
    listed.start()
    row = row_of()
    upper = row < 4
    flip = jnp.where(row % 2 == 0, 1.0, -1.0)

    def device(n):
        first = block_of(n)
        for i in range(20):
            four = tab[n, 4 * i : 4 * i + 4, :]
            at = pl.multiple_of(first + 8 * i, 8)
            tre[pl.ds(at, 8), :] = jnp.where(upper, across(four, 0), across(four, 2))
            tim[pl.ds(at, 8), :] = jnp.where(upper, across(four, 1), across(four, 3)) * flip

    repeat(16, 2, device)

    def interpolate(n):
        at = pl.multiple_of(n * 128, 128)
        rows = jnp.concatenate([win[n * 8 + q, :16, :] for q in range(8)], 0)
        full[pl.ds(at, 128), :] = product3(halves(rows), (w[:LANES], w[LANES:]), ((1,), (0,)))

    repeat(8, 4, interpolate)

    def aggregate(u):
        at = pl.multiple_of(u * 32, 32)
        lay = []
        for h in range(2):
            lanes = pl.ds(pl.multiple_of((2 * half + 1 + h) * LANES, LANES), LANES)
            straight = turned = 0.0
            for k in range(4):
                x = full[pl.ds(at + 8 * k, 8), h * LANES : (h + 1) * LANES]
                straight += spins[8 * k : 8 * k + 8, lanes] * x
                turned += spins[32 + 8 * k : 40 + 8 * k, lanes] * x
            total = straight + swap(turned)
            lay.append(total + pltpu.roll(total, 4, 0))
        pat[pl.ds(pl.multiple_of(u * 8, 8), 8), :] = jnp.where(upper, lay[0], lay[1])

    repeat(32, 4, aggregate)
    listed.wait()

    def translate(n):
        for q in range(2):
            u = 2 * n + q
            acc = jnp.zeros((8, LANES), F32)
            acc2 = jnp.zeros((8, LANES), F32)
            for e in range(16):
                x = pat[pl.ds(pl.multiple_of(scalars[u, e], 8), 8), :]
                op = pl.ds(pl.multiple_of(scalars[u, 16 + e], 8), 8)
                acc += tre[op, :] * x
                acc2 += tim[op, :] * x
            same[u], cross[u] = acc, acc2

    repeat(16, 2, translate)

    def border(n):
        for whole, rim, shift in ((own, rim_own, 0), (oth, rim_oth, 16)):
            one = same[2 * n + shift] + swap(cross[2 * n + shift])
            two = same[2 * n + 1 + shift] + swap(cross[2 * n + 1 + shift])
            whole[2 * n], whole[2 * n + 1] = one, two
            first = jnp.where(upper, one, pltpu.roll(two, 4, 0))
            last = jnp.where(upper, pltpu.roll(one, 4, 0), two)
            rim[n] = jnp.where(half == 0, first, last)

    repeat(8, 8, border)


def lower_kernel(sources, operators, win, tab, out, t8, pat, full, lists, scalars, sem):
    by_target = [jnp.transpose(x[...] * 8) for x in (sources, operators)]
    for q in range(4):
        for k in range(2):
            lists[:, 32 * q + 16 * k : 32 * q + 16 * k + 16] = by_target[k][32 * q : 32 * q + 32]
    listed = pltpu.make_async_copy(lists, scalars, sem)
    listed.start()
    row, lane = row_of(), lane_of()
    upper, lane_half = row < 4, lax.axis_index("box") * 96
    flip = jnp.where(upper | (row % 2 == 0), 1.0, -1.0)
    absent = (lane >= 96 - lane_half) & (lane < 128 - lane_half)

    def device(n):
        first = block_of(n)
        for i in range(20):
            two = tab[n, 80 + 2 * i : 82 + 2 * i, :]
            at = pl.multiple_of(first + 8 * i, 8)
            t8[pl.ds(at, 8), :] = jnp.where(upper, across(two, 0), across(two, 1)) * flip

    repeat(16, 2, device)
    def spread_out(n):
        extra = win[n, 16:24, :]
        for v, x in enumerate((extra, pltpu.roll(extra, 64, 1))):
            x = jnp.where(absent, x, win[n, 8 * v : 8 * v + 8, :])
            turned = pltpu.roll(x, 4, 0)
            at = pl.multiple_of(n * 32 + 16 * v, 8)
            pat[pl.ds(at, 8), :] = jnp.where(upper, x, turned)
            pat[pl.ds(at + 8, 8), :] = jnp.where(upper, turned, x)

    repeat(64, 8, spread_out)
    listed.wait()

    def four(n):
        for q in range(4):
            acc = [jnp.zeros((8, LANES), F32)] * 2
            for e in range(16):
                op = pl.ds(pl.multiple_of(scalars[n, 32 * q + 16 + e], 8), 8)
                src = pl.ds(pl.multiple_of(scalars[n, 32 * q + e], 8), 8)
                acc[e % 2] += t8[op, :] * pat[src, :]
            full[32 * q + n] = acc[0] + acc[1]

    repeat(32, 1, four)

    def fold(n):
        one, two = full[2 * n], full[2 * n + 1]
        same = jnp.where(upper, one, pltpu.roll(two, 4, 0))
        out[n] = same + swap(jnp.where(upper, pltpu.roll(one, 4, 0), two))

    repeat(64, 16, fold)


def final_kernel(
    own, got, rim_a, rim_b, low, m, spins, low_hbm, high_hbm, low_out, high_out, lh, ll, sem
):
    row = row_of()
    upper = row < 4
    first = lax.axis_index("box") == 0

    def pair(n):
        rims = (jnp.where(first, rim_b[n], rim_a[n]), jnp.where(first, rim_a[n], rim_b[n]))
        for q in range(2):
            u = 2 * n + q
            one = jnp.where(first, own[u], got[u])
            two = jnp.where(first, got[u], own[u])
            for jt, x in enumerate((one, one, two, two)):
                for r in range(2):
                    high_out[u, r, :, jt * LANES : (jt + 1) * LANES] = x[
                        4 * (jt % 2) + 2 * r : 4 * (jt % 2) + 2 * r + 2, :
                    ]
            blocks = []
            for x in (one, two):
                turned = pltpu.roll(x, 4, 0)
                blocks += [jnp.where(upper, x, turned), jnp.where(upper, turned, x)]
            edge = []
            for x in rims:
                turned = pltpu.roll(x, 4, 0)
                edge.append(jnp.where(upper, x, turned) if q == 0 else jnp.where(upper, turned, x))
            blocks = [edge[0]] + blocks + [edge[1]]
            at = pl.multiple_of(u * 32, 32)
            for jt, x in enumerate(blocks):
                lanes = slice(jt * LANES, (jt + 1) * LANES)
                y = swap(x)
                rows = jnp.concatenate(
                    [
                        spins[8 * g : 8 * g + 8, lanes] * x + spins[32 + 8 * g : 40 + 8 * g, lanes] * y
                        for g in range(4)
                    ],
                    0,
                )
                lh[pl.ds(at, 32), lanes], ll[pl.ds(at, 32), lanes] = halves(rows)

    repeat(8, 2, pair)

    copies = [pltpu.make_async_copy(high_out, high_hbm, sem.at[4])]
    copies[0].start()
    for n in range(4):
        at = slice(n * 128, (n + 1) * 128)
        sums = product3((lh[at, :], ll[at, :]), (m[:LANES, :], m[LANES:, :]), ((1,), (1,)))
        low_out[at, :] = sums + low[at, :]
        copies.append(pltpu.make_async_copy(low_out.at[at], low_hbm.at[at], sem.at[n]))
        copies[-1].start()
    for copy in copies:
        copy.wait()


def shards(
    radiated,
    low_table,
    high_table,
    low_sources,
    low_operators,
    high_sources,
    high_operators,
    stencil_index,
    stencil_weight,
    shift_angle,
):
    n_samp = lax.axis_size("samp")
    dma = pltpu.SemaphoreType.DMA
    (give,) = call(
        table_kernel,
        [HBM] * 4,
        [((SENT, LANES), F32)],
        [pltpu.VMEM((20, 2, LANES), F32), pltpu.VMEM((20, 2, 512), F32)]
        + [pltpu.VMEM((16, 16), I32)] * 2
        + [dma((4,))],
        moved=1 << 20,
        room=ALL_VMEM,
    )(low_table, high_table, high_sources, high_operators)
    got = lax.ppermute(give, "box", [(0, 1), (1, 0)])
    made = [
        ((64, 24, LANES), F32),
        ((256, 256), BF16),
        ((256, 768), BF16),
        ((80, 768), F32),
        ((2, ROWS, LANES), F32),
    ]
    win, w, m, spins, pair = call(
        ready_kernel,
        [HBM] * 8,
        made,
        [pltpu.VMEM((4, 2, 2, 4096), F32), pltpu.VMEM((16, 4096), F32), pltpu.VMEM(*made[0])]
        + [pltpu.VMEM((16, 768), I32), pltpu.VMEM((16, 768), F32), pltpu.VMEM((8, 768), F32)]
        + [pltpu.VMEM(*x) for x in made[1:4]]
        + [pltpu.VMEM((16, 16), I32)] * 2
        + [pltpu.VMEM((20, 2, LANES), F32), pltpu.VMEM((20, 2, 512), F32)]
        + [pltpu.VMEM((ROWS, LANES), F32), dma((14,)), dma((5,))],
        flops=10 << 20,
        moved=8 << 20,
        out_place=HBM,
        room=ALL_VMEM,
    )(radiated, stencil_index, stencil_weight, shift_angle, high_sources, high_operators, low_table, high_table)
    win, got = lax.optimization_barrier((win, got))
    win = lax.all_to_all(win, ("box", "samp"), 0, 0, tiled=True)
    tab = lax.all_gather(pair.at[1].set(got[:ROWS]), "rhs", tiled=True)
    part, rim = ((16, 8, LANES), F32), ((8, 8, LANES), F32)
    own, oth, rim_own, rim_oth = call(
        upper_kernel,
        [VMEM] * 5,
        [part, part, rim, rim],
        [
            pltpu.VMEM((2560, LANES), F32),
            pltpu.VMEM((2560, LANES), F32),
            pltpu.VMEM((1024, 256), F32),
            pltpu.VMEM((256, LANES), F32),
            pltpu.VMEM((32, 8, LANES), F32),
            pltpu.VMEM((32, 8, LANES), F32),
            pltpu.VMEM((32, LANES), I32),
            pltpu.SMEM((32, LANES), I32),
            dma,
        ],
        flops=200 << 20,
        moved=6 << 20,
    )(tab, got, win, w, spins)
    flat = lambda s, b: 2 * s + b
    other = lax.ppermute(oth, "box", [(0, 1), (1, 0)])
    down = [(flat(s, 0), s - 1) for s in range(1, n_samp)]
    up = [(flat(s, 1), s + 1) for s in range(n_samp - 1)]
    both = ("samp", "box")
    rim_a = lax.ppermute(
        rim_own, both, [(i, flat(s, 0)) for i, s in down] + [(i, flat(s, 1)) for i, s in up]
    )
    rim_b = lax.ppermute(
        rim_oth, both, [(i, flat(s, 1)) for i, s in down] + [(i, flat(s, 0)) for i, s in up]
    )
    (low,) = call(
        lower_kernel,
        [VMEM] * 4,
        [((64, 8, LANES), F32)],
        [
            pltpu.VMEM((2560, LANES), F32),
            pltpu.VMEM((2048, LANES), F32),
            pltpu.VMEM((LANES, 8, LANES), F32),
            pltpu.VMEM((32, LANES), I32),
            pltpu.SMEM((32, LANES), I32),
            dma,
        ],
        flops=20 << 20,
        moved=10 << 20,
    )(low_sources.T, low_operators.T, win, tab)
    low_incoming, high_incoming = call(
        final_kernel,
        [VMEM] * 7,
        [((512, LANES), F32), ((16, 2, 2, 512), F32)],
        [pltpu.VMEM((512, LANES), F32), pltpu.VMEM((16, 2, 2, 512), F32)]
        + [pltpu.VMEM((512, 768), BF16)] * 2
        + [dma((5,))],
        flops=300 << 20,
        moved=4 << 20,
        out_place=HBM,
    )(own, other, rim_a, rim_b, low.reshape(512, LANES), m, spins)
    return low_incoming.reshape(128, 2, 2, LANES), high_incoming


def solution(mesh):
    return jax.shard_map(
        shards,
        mesh=mesh,
        in_specs=(
            P(("box", "samp"), "rhs", None, None),
            P(("box", "rhs"), None, "samp"),
            P(("box", "rhs"), None, "samp"),
            P("box", None),
            P("box", None),
            P("box", None),
            P("box", None),
            P(),
            P(),
            P(),
        ),
        out_specs=(P("box", "rhs", None, "samp"), P("box", "rhs", None, "samp")),
        check_vma=False,
    )
```

```python
import jax
import jax.numpy as jnp
from jax import lax
from jax.experimental import pallas as pl
from jax.experimental.pallas import tpu as pltpu
from jax.sharding import PartitionSpec as P

F32, BF16, I32 = jnp.float32, jnp.bfloat16, jnp.int32
VMEM = pl.BlockSpec(memory_space=pltpu.VMEM)
SMEM = pl.BlockSpec(memory_space=pltpu.SMEM)
HBM = pl.BlockSpec(memory_space=pltpu.HBM)
LANES = 128
ROWS = 120
ALL_VMEM = 63 << 20
SENT = ROWS + 16


def call(kernel, ins, outs, scratch=(), flops=0, moved=0, out_place=VMEM, room=24 << 20):
    return pl.pallas_call(
        kernel,
        in_specs=list(ins),
        out_specs=[out_place] * len(outs),
        out_shape=[jax.ShapeDtypeStruct(s, d) for s, d in outs],
        scratch_shapes=list(scratch),
        compiler_params=pltpu.CompilerParams(vmem_limit_bytes=room),
        cost_estimate=pl.CostEstimate(flops=flops, bytes_accessed=moved, transcendentals=0),
    )


def halves(x):
    high = x.astype(BF16)
    return high, (x - high.astype(F32)).astype(BF16)


def row_of(shape=(8, LANES)):
    return lax.broadcasted_iota(I32, shape, 0)


def lane_of(shape=(8, LANES)):
    return lax.broadcasted_iota(I32, shape, 1)


def run_all(copies):
    for copy in copies:
        copy.start()
    for copy in copies:
        copy.wait()


def repeat(count, step, body):
    def several(n, carry):
        for i in range(step):
            body(n * step + i)
        return carry

    lax.fori_loop(0, count // step, several, 0)


def swap(x):
    return jnp.where(row_of() % 2 == 0, pltpu.roll(x, 7, 0), pltpu.roll(x, 1, 0))


def across(x, row):
    return jnp.broadcast_to(x[row : row + 1, :], (8, LANES))


def product3(left, right, dims):
    (lh, ll), (rh, rl) = left, right
    dot = lambda a, b: lax.dot_general(a, b, (dims, ((), ())), preferred_element_type=F32)
    return dot(lh, rh) + (dot(lh, rl) + dot(ll, rh))


def block_of(n):
    return (lax.bitwise_xor(n % 2, lax.axis_index("box")) * 8 + n // 2) * 160


def pack_tables(low, high, b, out):
    for op in range(20):
        for jh in range(2):
            lanes = pl.ds(pl.multiple_of((2 * b + jh) * LANES, LANES), LANES)
            at = 4 * op + 2 * jh
            out[at : at + 2, :] = high[op, :, lanes]
        out[80 + 2 * op : 82 + 2 * op, :] = low[op]


def table_kernel(
    low_hbm, high_hbm, sources_hbm, operators_hbm, give, low, high, sources, operators, sem
):
    run_all(
        [
            pltpu.make_async_copy(low_hbm, low, sem.at[0]),
            pltpu.make_async_copy(high_hbm, high, sem.at[1]),
            pltpu.make_async_copy(sources_hbm, sources, sem.at[2]),
            pltpu.make_async_copy(operators_hbm, operators, sem.at[3]),
        ]
    )
    pack_tables(low, high, 1 - lax.axis_index("box"), give)
    give[ROWS:, :] = jnp.zeros((16, LANES), F32)
    give[ROWS:, 0:16] = sources[...].astype(F32)
    give[ROWS:, 16:32] = operators[...].astype(F32)


def ready_kernel(
    rad_hbm, index, weight, angle, sources_hbm, operators_hbm, low_hbm, high_hbm,
    win_out, w_out, m_out, spin_out, pair_out,
    rad, rows, win, idx, wgt, ang, w, m, spins, sources, operators, low_own, high_own, keep, sem, out_sem,
):
    seg, half = lax.axis_index("samp"), lax.axis_index("box")
    start = pl.multiple_of(seg * 512, LANES)
    total = index.shape[1]
    before = pl.multiple_of(jnp.maximum(start - LANES, 0), LANES)
    after = pl.multiple_of(jnp.minimum(start + 512, total - LANES), LANES)
    first = pltpu.make_async_copy(rad_hbm, rad, sem.at[9])
    first.start()
    copies = []
    for n, (src, dst) in enumerate(((index, idx), (weight, wgt), (angle, ang))):
        for k, (at, to, width) in enumerate(((before, 0, 128), (start, 128, 512), (after, 640, 128))):
            copies.append(
                pltpu.make_async_copy(
                    src.at[:, pl.ds(at, width)], dst.at[:, to : to + width], sem.at[3 * n + k]
                )
            )
    copies.append(pltpu.make_async_copy(sources_hbm, sources, sem.at[10]))
    copies.append(pltpu.make_async_copy(operators_hbm, operators, sem.at[11]))
    copies.append(pltpu.make_async_copy(low_hbm, low_own, sem.at[12]))
    copies.append(pltpu.make_async_copy(high_hbm, high_own, sem.at[13]))
    for copy in copies:
        copy.start()
    first.wait()
    for o in range(4):
        for r in range(2):
            rows[4 * o + 2 * r : 4 * o + 2 * r + 2, :] = rad[o, r]
    n_samp = rows.shape[1] // LANES
    lane = lane_of((16, LANES))
    lane8 = lane_of()
    block = lambda s: rows[:, (s % n_samp) * LANES : (s % n_samp + 1) * LANES]
    for s in range(n_samp):
        here = block(s)
        near_rows, far_rows = here[:8], pltpu.roll(here[8:], 64, 1)
        for b, near, low, rest in ((0, s - 1, 0, 96), (1, s + 1, 32, 128)):
            inside = (lane >= low) & (lane < rest)
            inside8 = (lane8 >= low) & (lane8 < rest)
            win[b * n_samp + s, :16, :] = jnp.where(inside, here, block(near))
            win[b * n_samp + s, 16:, :] = jnp.where(inside8, far_rows, near_rows)
    last = [pltpu.make_async_copy(win, win_out, out_sem.at[0])]
    last[0].start()
    for copy in copies:
        copy.wait()

    def band(at, first, low=0, rest=LANES):
        found = idx[:, pl.ds(at, LANES)]
        found = found & 127 if first is None else found - first
        value = wgt[:, pl.ds(at, LANES)]
        matrix = jnp.zeros((rest - low, LANES), F32)
        slot = row_of((rest - low, LANES)) + low
        for p in range(16):
            matrix += jnp.where(found[p : p + 1, :] == slot, value[p : p + 1, :], 0.0)
        return halves(matrix)

    own = pl.multiple_of(LANES + 256 * half, LANES)

    cosine, sine = jnp.cos(ang[...]), jnp.sin(ang[...])
    spin = jnp.where(row_of((4, 768)) % 2 == 0, 1.0, -1.0)
    spins[:32, :] = jnp.concatenate(
        [jnp.broadcast_to(cosine[o : o + 1], (4, 768)) for o in range(8)], 0
    )
    spins[32:64, :] = jnp.concatenate(
        [jnp.broadcast_to(sine[o : o + 1], (4, 768)) * spin for o in range(8)], 0
    )
    spins[64:, :] = jnp.zeros((16, 768), F32)
    spins[64:, 0:16] = sources[...].astype(F32)
    spins[64:, 16:32] = operators[...].astype(F32)

    def send(src, dst):
        last.append(pltpu.make_async_copy(src, dst, out_sem.at[len(last)]))
        last[-1].start()

    send(spins, spin_out)
    pack_tables(low_own, high_own, half, keep)
    send(keep, pair_out.at[0])
    for n in range(2):
        lanes = slice(n * LANES, (n + 1) * LANES)
        w[:LANES, lanes], w[LANES:, lanes] = band(
            pl.multiple_of(own + n * LANES, LANES), None
        )
    send(w, w_out)
    m[...] = jnp.zeros_like(m)
    for n in range(6):
        lanes, low, rest = slice(n * LANES, (n + 1) * LANES), max(32 * n - 64, 0), min(32 * n + 32, LANES)
        m[low:rest, lanes], m[LANES + low : LANES + rest, lanes] = band(
            n * LANES, seg * 128, low, rest
        )
    send(m, m_out)
    for copy in last:
        copy.wait()


def upper_kernel(
    tab, got, win, w, spins,
    own, oth, rim_own, rim_oth,
    tre, tim, full, pat, same, cross, lists, scalars, sem,
):
    half = lax.axis_index("box")
    lists[:16, :] = (spins[64:, :LANES] * 8.0).astype(I32)
    lists[16:, :] = (got[ROWS:, :] * 8.0).astype(I32)
    listed = pltpu.make_async_copy(lists, scalars, sem)
    listed.start()
    row = row_of()
    upper = row < 4
    flip = jnp.where(row % 2 == 0, 1.0, -1.0)

    def device(n):
        first = block_of(n)
        for i in range(20):
            four = tab[n, 4 * i : 4 * i + 4, :]
            at = pl.multiple_of(first + 8 * i, 8)
            tre[pl.ds(at, 8), :] = jnp.where(upper, across(four, 0), across(four, 2))
            tim[pl.ds(at, 8), :] = jnp.where(upper, across(four, 1), across(four, 3)) * flip

    repeat(16, 2, device)

    def interpolate(n):
        at = pl.multiple_of(n * 128, 128)
        rows = jnp.concatenate([win[n * 8 + q, :16, :] for q in range(8)], 0)
        full[pl.ds(at, 128), :] = product3(halves(rows), (w[:LANES], w[LANES:]), ((1,), (0,)))

    repeat(8, 8, interpolate)

    def aggregate(u):
        at = pl.multiple_of(u * 32, 32)
        lay = []
        for h in range(2):
            lanes = pl.ds(pl.multiple_of((2 * half + 1 + h) * LANES, LANES), LANES)
            straight = turned = 0.0
            for k in range(4):
                x = full[pl.ds(at + 8 * k, 8), h * LANES : (h + 1) * LANES]
                straight += spins[8 * k : 8 * k + 8, lanes] * x
                turned += spins[32 + 8 * k : 40 + 8 * k, lanes] * x
            total = straight + swap(turned)
            lay.append(total + pltpu.roll(total, 4, 0))
        pat[pl.ds(pl.multiple_of(u * 8, 8), 8), :] = jnp.where(upper, lay[0], lay[1])

    repeat(32, 8, aggregate)
    listed.wait()

    def translate(n):
        for q in range(2):
            u = 2 * n + q
            acc = jnp.zeros((8, LANES), F32)
            acc2 = jnp.zeros((8, LANES), F32)
            for e in range(16):
                x = pat[pl.ds(pl.multiple_of(scalars[u, e], 8), 8), :]
                op = pl.ds(pl.multiple_of(scalars[u, 16 + e], 8), 8)
                acc += tre[op, :] * x
                acc2 += tim[op, :] * x
            same[u], cross[u] = acc, acc2

    repeat(16, 4, translate)

    def border(n):
        for whole, rim, shift in ((own, rim_own, 0), (oth, rim_oth, 16)):
            one = same[2 * n + shift] + swap(cross[2 * n + shift])
            two = same[2 * n + 1 + shift] + swap(cross[2 * n + 1 + shift])
            whole[2 * n], whole[2 * n + 1] = one, two
            first = jnp.where(upper, one, pltpu.roll(two, 4, 0))
            last = jnp.where(upper, pltpu.roll(one, 4, 0), two)
            rim[n] = jnp.where(half == 0, first, last)

    repeat(8, 8, border)


def lower_kernel(sources, operators, win, tab, out, t8, pat, full, lists, scalars, sem):
    by_target = [jnp.transpose(x[...] * 8) for x in (sources, operators)]
    for q in range(4):
        for k in range(2):
            lists[:, 32 * q + 16 * k : 32 * q + 16 * k + 16] = by_target[k][32 * q : 32 * q + 32]
    listed = pltpu.make_async_copy(lists, scalars, sem)
    listed.start()
    row, lane = row_of(), lane_of()
    upper, lane_half = row < 4, lax.axis_index("box") * 96
    flip = jnp.where(upper | (row % 2 == 0), 1.0, -1.0)
    absent = (lane >= 96 - lane_half) & (lane < 128 - lane_half)

    def device(n):
        first = block_of(n)
        for i in range(20):
            two = tab[n, 80 + 2 * i : 82 + 2 * i, :]
            at = pl.multiple_of(first + 8 * i, 8)
            t8[pl.ds(at, 8), :] = jnp.where(upper, across(two, 0), across(two, 1)) * flip

    repeat(16, 2, device)
    def spread_out(n):
        extra = win[n, 16:24, :]
        for v, x in enumerate((extra, pltpu.roll(extra, 64, 1))):
            x = jnp.where(absent, x, win[n, 8 * v : 8 * v + 8, :])
            turned = pltpu.roll(x, 4, 0)
            at = pl.multiple_of(n * 32 + 16 * v, 8)
            pat[pl.ds(at, 8), :] = jnp.where(upper, x, turned)
            pat[pl.ds(at + 8, 8), :] = jnp.where(upper, turned, x)

    repeat(64, 8, spread_out)
    listed.wait()

    def four(n):
        for q in range(4):
            acc = [jnp.zeros((8, LANES), F32)] * 2
            for e in range(16):
                op = pl.ds(pl.multiple_of(scalars[n, 32 * q + 16 + e], 8), 8)
                src = pl.ds(pl.multiple_of(scalars[n, 32 * q + e], 8), 8)
                acc[e % 2] += t8[op, :] * pat[src, :]
            full[32 * q + n] = acc[0] + acc[1]

    repeat(32, 4, four)

    def fold(n):
        one, two = full[2 * n], full[2 * n + 1]
        same = jnp.where(upper, one, pltpu.roll(two, 4, 0))
        out[n] = same + swap(jnp.where(upper, pltpu.roll(one, 4, 0), two))

    repeat(64, 16, fold)


def final_kernel(
    own, got, rim_a, rim_b, low, m, spins, low_hbm, high_hbm, low_out, high_out, lh, ll, sem
):
    row = row_of()
    upper = row < 4
    first = lax.axis_index("box") == 0

    def pair(n):
        rims = (jnp.where(first, rim_b[n], rim_a[n]), jnp.where(first, rim_a[n], rim_b[n]))
        for q in range(2):
            u = 2 * n + q
            one = jnp.where(first, own[u], got[u])
            two = jnp.where(first, got[u], own[u])
            for jt, x in enumerate((one, one, two, two)):
                for r in range(2):
                    high_out[u, r, :, jt * LANES : (jt + 1) * LANES] = x[
                        4 * (jt % 2) + 2 * r : 4 * (jt % 2) + 2 * r + 2, :
                    ]
            blocks = []
            for x in (one, two):
                turned = pltpu.roll(x, 4, 0)
                blocks += [jnp.where(upper, x, turned), jnp.where(upper, turned, x)]
            edge = []
            for x in rims:
                turned = pltpu.roll(x, 4, 0)
                edge.append(jnp.where(upper, x, turned) if q == 0 else jnp.where(upper, turned, x))
            blocks = [edge[0]] + blocks + [edge[1]]
            at = pl.multiple_of(u * 32, 32)
            for jt, x in enumerate(blocks):
                lanes = slice(jt * LANES, (jt + 1) * LANES)
                y = swap(x)
                rows = jnp.concatenate(
                    [
                        spins[8 * g : 8 * g + 8, lanes] * x + spins[32 + 8 * g : 40 + 8 * g, lanes] * y
                        for g in range(4)
                    ],
                    0,
                )
                lh[pl.ds(at, 32), lanes], ll[pl.ds(at, 32), lanes] = halves(rows)

    repeat(8, 4, pair)

    copies = [pltpu.make_async_copy(high_out, high_hbm, sem.at[4])]
    copies[0].start()
    for n in range(4):
        at = slice(n * 128, (n + 1) * 128)
        sums = product3((lh[at, :], ll[at, :]), (m[:LANES, :], m[LANES:, :]), ((1,), (1,)))
        low_out[at, :] = sums + low[at, :]
        copies.append(pltpu.make_async_copy(low_out.at[at], low_hbm.at[at], sem.at[n]))
        copies[-1].start()
    for copy in copies:
        copy.wait()


def shards(
    radiated,
    low_table,
    high_table,
    low_sources,
    low_operators,
    high_sources,
    high_operators,
    stencil_index,
    stencil_weight,
    shift_angle,
):
    n_samp = lax.axis_size("samp")
    dma = pltpu.SemaphoreType.DMA
    (give,) = call(
        table_kernel,
        [HBM] * 4,
        [((SENT, LANES), F32)],
        [pltpu.VMEM((20, 2, LANES), F32), pltpu.VMEM((20, 2, 512), F32)]
        + [pltpu.VMEM((16, 16), I32)] * 2
        + [dma((4,))],
        moved=1 << 20,
        room=ALL_VMEM,
    )(low_table, high_table, high_sources, high_operators)
    got = lax.ppermute(give, "box", [(0, 1), (1, 0)])
    made = [
        ((64, 24, LANES), F32),
        ((256, 256), BF16),
        ((256, 768), BF16),
        ((80, 768), F32),
        ((2, ROWS, LANES), F32),
    ]
    win, w, m, spins, pair = call(
        ready_kernel,
        [HBM] * 8,
        made,
        [pltpu.VMEM((4, 2, 2, 4096), F32), pltpu.VMEM((16, 4096), F32), pltpu.VMEM(*made[0])]
        + [pltpu.VMEM((16, 768), I32), pltpu.VMEM((16, 768), F32), pltpu.VMEM((8, 768), F32)]
        + [pltpu.VMEM(*x) for x in made[1:4]]
        + [pltpu.VMEM((16, 16), I32)] * 2
        + [pltpu.VMEM((20, 2, LANES), F32), pltpu.VMEM((20, 2, 512), F32)]
        + [pltpu.VMEM((ROWS, LANES), F32), dma((14,)), dma((5,))],
        flops=10 << 20,
        moved=8 << 20,
        out_place=HBM,
        room=ALL_VMEM,
    )(radiated, stencil_index, stencil_weight, shift_angle, high_sources, high_operators, low_table, high_table)
    win, got = lax.optimization_barrier((win, got))
    win = lax.all_to_all(win, ("box", "samp"), 0, 0, tiled=True)
    tab = lax.all_gather(
        pair.at[1].set(got[:ROWS]).reshape(2 * ROWS, LANES), "rhs", tiled=True
    ).reshape(16, ROWS, LANES)
    part, rim = ((16, 8, LANES), F32), ((8, 8, LANES), F32)
    own, oth, rim_own, rim_oth = call(
        upper_kernel,
        [VMEM] * 5,
        [part, part, rim, rim],
        [
            pltpu.VMEM((2560, LANES), F32),
            pltpu.VMEM((2560, LANES), F32),
            pltpu.VMEM((1024, 256), F32),
            pltpu.VMEM((256, LANES), F32),
            pltpu.VMEM((32, 8, LANES), F32),
            pltpu.VMEM((32, 8, LANES), F32),
            pltpu.VMEM((32, LANES), I32),
            pltpu.SMEM((32, LANES), I32),
            dma,
        ],
        flops=200 << 20,
        moved=6 << 20,
    )(tab, got, win, w, spins)
    flat = lambda s, b: 2 * s + b
    other = lax.ppermute(oth, "box", [(0, 1), (1, 0)])
    down = [(flat(s, 0), s - 1) for s in range(1, n_samp)]
    up = [(flat(s, 1), s + 1) for s in range(n_samp - 1)]
    both = ("samp", "box")
    rim_a = lax.ppermute(
        rim_own, both, [(i, flat(s, 0)) for i, s in down] + [(i, flat(s, 1)) for i, s in up]
    )
    rim_b = lax.ppermute(
        rim_oth, both, [(i, flat(s, 1)) for i, s in down] + [(i, flat(s, 0)) for i, s in up]
    )
    (low,) = call(
        lower_kernel,
        [VMEM] * 4,
        [((64, 8, LANES), F32)],
        [
            pltpu.VMEM((2560, LANES), F32),
            pltpu.VMEM((2048, LANES), F32),
            pltpu.VMEM((LANES, 8, LANES), F32),
            pltpu.VMEM((32, LANES), I32),
            pltpu.SMEM((32, LANES), I32),
            dma,
        ],
        flops=20 << 20,
        moved=10 << 20,
    )(low_sources.T, low_operators.T, win, tab)
    low_incoming, high_incoming = call(
        final_kernel,
        [VMEM] * 7,
        [((512, LANES), F32), ((16, 2, 2, 512), F32)],
        [pltpu.VMEM((512, LANES), F32), pltpu.VMEM((16, 2, 2, 512), F32)]
        + [pltpu.VMEM((512, 768), BF16)] * 2
        + [dma((5,))],
        flops=300 << 20,
        moved=4 << 20,
        out_place=HBM,
    )(own, other, rim_a, rim_b, low.reshape(512, LANES), m, spins)
    return low_incoming.reshape(128, 2, 2, LANES), high_incoming


def solution(mesh):
    return jax.shard_map(
        shards,
        mesh=mesh,
        in_specs=(
            P(("box", "samp"), "rhs", None, None),
            P(("box", "rhs"), None, "samp"),
            P(("box", "rhs"), None, "samp"),
            P("box", None),
            P("box", None),
            P("box", None),
            P("box", None),
            P(),
            P(),
            P(),
        ),
        out_specs=(P("box", "rhs", None, "samp"), P("box", "rhs", None, "samp")),
        check_vma=False,
    )
```

```python
import jax
import jax.numpy as jnp
from jax import lax
from jax.experimental import pallas as pl
from jax.experimental.pallas import tpu as pltpu
from jax.sharding import PartitionSpec as P

F32, BF16, I32 = jnp.float32, jnp.bfloat16, jnp.int32
VMEM = pl.BlockSpec(memory_space=pltpu.VMEM)
SMEM = pl.BlockSpec(memory_space=pltpu.SMEM)
HBM = pl.BlockSpec(memory_space=pltpu.HBM)
LANES = 128
ROWS = 120
ALL_VMEM = 63 << 20
SENT = ROWS + 16


def call(kernel, ins, outs, scratch=(), flops=0, moved=0, out_place=VMEM, room=24 << 20):
    return pl.pallas_call(
        kernel,
        in_specs=list(ins),
        out_specs=[out_place] * len(outs),
        out_shape=[jax.ShapeDtypeStruct(s, d) for s, d in outs],
        scratch_shapes=list(scratch),
        compiler_params=pltpu.CompilerParams(vmem_limit_bytes=room),
        cost_estimate=pl.CostEstimate(flops=flops, bytes_accessed=moved, transcendentals=0),
    )


def halves(x):
    high = x.astype(BF16)
    return high, (x - high.astype(F32)).astype(BF16)


def row_of(shape=(8, LANES)):
    return lax.broadcasted_iota(I32, shape, 0)


def lane_of(shape=(8, LANES)):
    return lax.broadcasted_iota(I32, shape, 1)


def run_all(copies):
    for copy in copies:
        copy.start()
    for copy in copies:
        copy.wait()


def repeat(count, step, body):
    def several(n, carry):
        for i in range(step):
            body(n * step + i)
        return carry

    lax.fori_loop(0, count // step, several, 0)


def swap(x):
    return jnp.where(row_of() % 2 == 0, pltpu.roll(x, 7, 0), pltpu.roll(x, 1, 0))


def across(x, row):
    return jnp.broadcast_to(x[row : row + 1, :], (8, LANES))


def product3(left, right, dims):
    (lh, ll), (rh, rl) = left, right
    dot = lambda a, b: lax.dot_general(a, b, (dims, ((), ())), preferred_element_type=F32)
    return dot(lh, rh) + (dot(lh, rl) + dot(ll, rh))


def block_of(n):
    return (lax.bitwise_xor(n % 2, lax.axis_index("box")) * 8 + n // 2) * 160


def pack_tables(low, high, b, out):
    for op in range(20):
        for jh in range(2):
            lanes = pl.ds(pl.multiple_of((2 * b + jh) * LANES, LANES), LANES)
            at = 4 * op + 2 * jh
            out[at : at + 2, :] = high[op, :, lanes]
        out[80 + 2 * op : 82 + 2 * op, :] = low[op]


def table_kernel(
    low_hbm, high_hbm, sources_hbm, operators_hbm, give, low, high, sources, operators, sem
):
    run_all(
        [
            pltpu.make_async_copy(low_hbm, low, sem.at[0]),
            pltpu.make_async_copy(high_hbm, high, sem.at[1]),
            pltpu.make_async_copy(sources_hbm, sources, sem.at[2]),
            pltpu.make_async_copy(operators_hbm, operators, sem.at[3]),
        ]
    )
    pack_tables(low, high, 1 - lax.axis_index("box"), give)
    give[ROWS:, :] = jnp.zeros((16, LANES), F32)
    give[ROWS:, 0:16] = sources[...].astype(F32)
    give[ROWS:, 16:32] = operators[...].astype(F32)


def ready_kernel(
    rad_hbm, index, weight, angle, sources_hbm, operators_hbm, low_hbm, high_hbm,
    win_out, w_out, m_out, spin_out, pair_out,
    rad, rows, win, idx, wgt, ang, w, m, spins, sources, operators, low_own, high_own, keep, sem, out_sem,
):
    seg, half = lax.axis_index("samp"), lax.axis_index("box")
    start = pl.multiple_of(seg * 512, LANES)
    total = index.shape[1]
    before = pl.multiple_of(jnp.maximum(start - LANES, 0), LANES)
    after = pl.multiple_of(jnp.minimum(start + 512, total - LANES), LANES)
    first = pltpu.make_async_copy(rad_hbm, rad, sem.at[9])
    first.start()
    copies = []
    for n, (src, dst) in enumerate(((index, idx), (weight, wgt), (angle, ang))):
        for k, (at, to, width) in enumerate(((before, 0, 128), (start, 128, 512), (after, 640, 128))):
            copies.append(
                pltpu.make_async_copy(
                    src.at[:, pl.ds(at, width)], dst.at[:, to : to + width], sem.at[3 * n + k]
                )
            )
    copies.append(pltpu.make_async_copy(sources_hbm, sources, sem.at[10]))
    copies.append(pltpu.make_async_copy(operators_hbm, operators, sem.at[11]))
    copies.append(pltpu.make_async_copy(low_hbm, low_own, sem.at[12]))
    copies.append(pltpu.make_async_copy(high_hbm, high_own, sem.at[13]))
    for copy in copies:
        copy.start()
    first.wait()
    for o in range(4):
        for r in range(2):
            rows[4 * o + 2 * r : 4 * o + 2 * r + 2, :] = rad[o, r]
    n_samp = rows.shape[1] // LANES
    lane = lane_of((16, LANES))
    lane8 = lane_of()
    block = lambda s: rows[:, (s % n_samp) * LANES : (s % n_samp + 1) * LANES]
    for s in range(n_samp):
        here = block(s)
        near_rows, far_rows = here[:8], pltpu.roll(here[8:], 64, 1)
        for b, near, low, rest in ((0, s - 1, 0, 96), (1, s + 1, 32, 128)):
            inside = (lane >= low) & (lane < rest)
            inside8 = (lane8 >= low) & (lane8 < rest)
            win[b * n_samp + s, :16, :] = jnp.where(inside, here, block(near))
            win[b * n_samp + s, 16:, :] = jnp.where(inside8, far_rows, near_rows)
    last = [pltpu.make_async_copy(win, win_out, out_sem.at[0])]
    last[0].start()
    for copy in copies:
        copy.wait()

    def band(at, first, low=0, rest=LANES):
        found = idx[:, pl.ds(at, LANES)]
        found = found & 127 if first is None else found - first
        value = wgt[:, pl.ds(at, LANES)]
        matrix = jnp.zeros((rest - low, LANES), F32)
        slot = row_of((rest - low, LANES)) + low
        for p in range(16):
            matrix += jnp.where(found[p : p + 1, :] == slot, value[p : p + 1, :], 0.0)
        return halves(matrix)

    own = pl.multiple_of(LANES + 256 * half, LANES)

    cosine, sine = jnp.cos(ang[...]), jnp.sin(ang[...])
    spin = jnp.where(row_of((4, 768)) % 2 == 0, 1.0, -1.0)
    spins[:32, :] = jnp.concatenate(
        [jnp.broadcast_to(cosine[o : o + 1], (4, 768)) for o in range(8)], 0
    )
    spins[32:64, :] = jnp.concatenate(
        [jnp.broadcast_to(sine[o : o + 1], (4, 768)) * spin for o in range(8)], 0
    )
    spins[64:, :] = jnp.zeros((16, 768), F32)
    spins[64:, 0:16] = sources[...].astype(F32)
    spins[64:, 16:32] = operators[...].astype(F32)

    def send(src, dst):
        last.append(pltpu.make_async_copy(src, dst, out_sem.at[len(last)]))
        last[-1].start()

    send(spins, spin_out)
    pack_tables(low_own, high_own, half, keep)
    send(keep, pair_out.at[0])
    for n in range(2):
        lanes = slice(n * LANES, (n + 1) * LANES)
        w[:LANES, lanes], w[LANES:, lanes] = band(
            pl.multiple_of(own + n * LANES, LANES), None
        )
    send(w, w_out)
    m[...] = jnp.zeros_like(m)
    for n in range(6):
        lanes, low, rest = slice(n * LANES, (n + 1) * LANES), max(32 * n - 64, 0), min(32 * n + 32, LANES)
        m[low:rest, lanes], m[LANES + low : LANES + rest, lanes] = band(
            n * LANES, seg * 128, low, rest
        )
    send(m, m_out)
    for copy in last:
        copy.wait()


def upper_kernel(
    tab, got, win, w, spins,
    own, oth, rim_own, rim_oth,
    tre, tim, full, pat, same, cross, lists, scalars, sem,
):
    half = lax.axis_index("box")
    lists[:16, :] = (spins[64:, :LANES] * 8.0).astype(I32)
    lists[16:, :] = (got[ROWS:, :] * 8.0).astype(I32)
    listed = pltpu.make_async_copy(lists, scalars, sem)
    listed.start()
    row = row_of()
    upper = row < 4
    flip = jnp.where(row % 2 == 0, 1.0, -1.0)

    def device(n):
        first = block_of(n)
        for i in range(20):
            four = tab[n, 4 * i : 4 * i + 4, :]
            at = pl.multiple_of(first + 8 * i, 8)
            tre[pl.ds(at, 8), :] = jnp.where(upper, across(four, 0), across(four, 2))
            tim[pl.ds(at, 8), :] = jnp.where(upper, across(four, 1), across(four, 3)) * flip

    repeat(16, 4, device)

    def interpolate(n):
        at = pl.multiple_of(n * 128, 128)
        rows = jnp.concatenate([win[n * 8 + q, :16, :] for q in range(8)], 0)
        full[pl.ds(at, 128), :] = product3(halves(rows), (w[:LANES], w[LANES:]), ((1,), (0,)))

    repeat(8, 8, interpolate)

    def aggregate(u):
        at = pl.multiple_of(u * 32, 32)
        lay = []
        for h in range(2):
            lanes = pl.ds(pl.multiple_of((2 * half + 1 + h) * LANES, LANES), LANES)
            straight = turned = 0.0
            for k in range(4):
                x = full[pl.ds(at + 8 * k, 8), h * LANES : (h + 1) * LANES]
                straight += spins[8 * k : 8 * k + 8, lanes] * x
                turned += spins[32 + 8 * k : 40 + 8 * k, lanes] * x
            total = straight + swap(turned)
            lay.append(total + pltpu.roll(total, 4, 0))
        pat[pl.ds(pl.multiple_of(u * 8, 8), 8), :] = jnp.where(upper, lay[0], lay[1])

    repeat(32, 16, aggregate)
    listed.wait()

    def translate(n):
        for q in range(2):
            u = 2 * n + q
            acc = jnp.zeros((8, LANES), F32)
            acc2 = jnp.zeros((8, LANES), F32)
            for e in range(16):
                x = pat[pl.ds(pl.multiple_of(scalars[u, e], 8), 8), :]
                op = pl.ds(pl.multiple_of(scalars[u, 16 + e], 8), 8)
                acc += tre[op, :] * x
                acc2 += tim[op, :] * x
            same[u], cross[u] = acc, acc2

    repeat(16, 8, translate)

    def border(n):
        for whole, rim, shift in ((own, rim_own, 0), (oth, rim_oth, 16)):
            one = same[2 * n + shift] + swap(cross[2 * n + shift])
            two = same[2 * n + 1 + shift] + swap(cross[2 * n + 1 + shift])
            whole[2 * n], whole[2 * n + 1] = one, two
            first = jnp.where(upper, one, pltpu.roll(two, 4, 0))
            last = jnp.where(upper, pltpu.roll(one, 4, 0), two)
            rim[n] = jnp.where(half == 0, first, last)

    repeat(8, 8, border)


def lower_kernel(sources, operators, win, tab, out, t8, pat, full, lists, scalars, sem):
    by_target = [jnp.transpose(x[...] * 8) for x in (sources, operators)]
    for q in range(4):
        for k in range(2):
            lists[:, 32 * q + 16 * k : 32 * q + 16 * k + 16] = by_target[k][32 * q : 32 * q + 32]
    listed = pltpu.make_async_copy(lists, scalars, sem)
    listed.start()
    row, lane = row_of(), lane_of()
    upper, lane_half = row < 4, lax.axis_index("box") * 96
    flip = jnp.where(upper | (row % 2 == 0), 1.0, -1.0)
    absent = (lane >= 96 - lane_half) & (lane < 128 - lane_half)

    def device(n):
        first = block_of(n)
        for i in range(20):
            two = tab[n, 80 + 2 * i : 82 + 2 * i, :]
            at = pl.multiple_of(first + 8 * i, 8)
            t8[pl.ds(at, 8), :] = jnp.where(upper, across(two, 0), across(two, 1)) * flip

    repeat(16, 4, device)
    def spread_out(n):
        extra = win[n, 16:24, :]
        for v, x in enumerate((extra, pltpu.roll(extra, 64, 1))):
            x = jnp.where(absent, x, win[n, 8 * v : 8 * v + 8, :])
            turned = pltpu.roll(x, 4, 0)
            at = pl.multiple_of(n * 32 + 16 * v, 8)
            pat[pl.ds(at, 8), :] = jnp.where(upper, x, turned)
            pat[pl.ds(at + 8, 8), :] = jnp.where(upper, turned, x)

    repeat(64, 8, spread_out)
    listed.wait()

    def four(n):
        for q in range(4):
            acc = [jnp.zeros((8, LANES), F32)] * 2
            for e in range(16):
                op = pl.ds(pl.multiple_of(scalars[n, 32 * q + 16 + e], 8), 8)
                src = pl.ds(pl.multiple_of(scalars[n, 32 * q + e], 8), 8)
                acc[e % 2] += t8[op, :] * pat[src, :]
            full[32 * q + n] = acc[0] + acc[1]

    repeat(32, 8, four)

    def fold(n):
        one, two = full[2 * n], full[2 * n + 1]
        same = jnp.where(upper, one, pltpu.roll(two, 4, 0))
        out[n] = same + swap(jnp.where(upper, pltpu.roll(one, 4, 0), two))

    repeat(64, 16, fold)


def final_kernel(
    own, got, rim_a, rim_b, low, m, spins, low_hbm, high_hbm, low_out, high_out, lh, ll, sem
):
    row = row_of()
    upper = row < 4
    first = lax.axis_index("box") == 0

    def pair(n):
        rims = (jnp.where(first, rim_b[n], rim_a[n]), jnp.where(first, rim_a[n], rim_b[n]))
        for q in range(2):
            u = 2 * n + q
            one = jnp.where(first, own[u], got[u])
            two = jnp.where(first, got[u], own[u])
            for jt, x in enumerate((one, one, two, two)):
                for r in range(2):
                    high_out[u, r, :, jt * LANES : (jt + 1) * LANES] = x[
                        4 * (jt % 2) + 2 * r : 4 * (jt % 2) + 2 * r + 2, :
                    ]
            blocks = []
            for x in (one, two):
                turned = pltpu.roll(x, 4, 0)
                blocks += [jnp.where(upper, x, turned), jnp.where(upper, turned, x)]
            edge = []
            for x in rims:
                turned = pltpu.roll(x, 4, 0)
                edge.append(jnp.where(upper, x, turned) if q == 0 else jnp.where(upper, turned, x))
            blocks = [edge[0]] + blocks + [edge[1]]
            at = pl.multiple_of(u * 32, 32)
            for jt, x in enumerate(blocks):
                lanes = slice(jt * LANES, (jt + 1) * LANES)
                y = swap(x)
                rows = jnp.concatenate(
                    [
                        spins[8 * g : 8 * g + 8, lanes] * x + spins[32 + 8 * g : 40 + 8 * g, lanes] * y
                        for g in range(4)
                    ],
                    0,
                )
                lh[pl.ds(at, 32), lanes], ll[pl.ds(at, 32), lanes] = halves(rows)

    repeat(8, 8, pair)

    copies = [pltpu.make_async_copy(high_out, high_hbm, sem.at[4])]
    copies[0].start()
    for n in range(4):
        at = slice(n * 128, (n + 1) * 128)
        sums = product3((lh[at, :], ll[at, :]), (m[:LANES, :], m[LANES:, :]), ((1,), (1,)))
        low_out[at, :] = sums + low[at, :]
        copies.append(pltpu.make_async_copy(low_out.at[at], low_hbm.at[at], sem.at[n]))
        copies[-1].start()
    for copy in copies:
        copy.wait()


def shards(
    radiated,
    low_table,
    high_table,
    low_sources,
    low_operators,
    high_sources,
    high_operators,
    stencil_index,
    stencil_weight,
    shift_angle,
):
    n_samp = lax.axis_size("samp")
    dma = pltpu.SemaphoreType.DMA
    (give,) = call(
        table_kernel,
        [HBM] * 4,
        [((SENT, LANES), F32)],
        [pltpu.VMEM((20, 2, LANES), F32), pltpu.VMEM((20, 2, 512), F32)]
        + [pltpu.VMEM((16, 16), I32)] * 2
        + [dma((4,))],
        moved=1 << 20,
        room=ALL_VMEM,
    )(low_table, high_table, high_sources, high_operators)
    got = lax.ppermute(give, "box", [(0, 1), (1, 0)])
    made = [
        ((64, 24, LANES), F32),
        ((256, 256), BF16),
        ((256, 768), BF16),
        ((80, 768), F32),
        ((2, ROWS, LANES), F32),
    ]
    win, w, m, spins, pair = call(
        ready_kernel,
        [HBM] * 8,
        made,
        [pltpu.VMEM((4, 2, 2, 4096), F32), pltpu.VMEM((16, 4096), F32), pltpu.VMEM(*made[0])]
        + [pltpu.VMEM((16, 768), I32), pltpu.VMEM((16, 768), F32), pltpu.VMEM((8, 768), F32)]
        + [pltpu.VMEM(*x) for x in made[1:4]]
        + [pltpu.VMEM((16, 16), I32)] * 2
        + [pltpu.VMEM((20, 2, LANES), F32), pltpu.VMEM((20, 2, 512), F32)]
        + [pltpu.VMEM((ROWS, LANES), F32), dma((14,)), dma((5,))],
        flops=10 << 20,
        moved=8 << 20,
        out_place=HBM,
        room=ALL_VMEM,
    )(radiated, stencil_index, stencil_weight, shift_angle, high_sources, high_operators, low_table, high_table)
    win, got = lax.optimization_barrier((win, got))
    win = lax.all_to_all(win, ("box", "samp"), 0, 0, tiled=True)
    tab = lax.all_gather(
        pair.at[1].set(got[:ROWS]).reshape(2 * ROWS, LANES), "rhs", tiled=True
    ).reshape(16, ROWS, LANES)
    part, rim = ((16, 8, LANES), F32), ((8, 8, LANES), F32)
    own, oth, rim_own, rim_oth = call(
        upper_kernel,
        [VMEM] * 5,
        [part, part, rim, rim],
        [
            pltpu.VMEM((2560, LANES), F32),
            pltpu.VMEM((2560, LANES), F32),
            pltpu.VMEM((1024, 256), F32),
            pltpu.VMEM((256, LANES), F32),
            pltpu.VMEM((32, 8, LANES), F32),
            pltpu.VMEM((32, 8, LANES), F32),
            pltpu.VMEM((32, LANES), I32),
            pltpu.SMEM((32, LANES), I32),
            dma,
        ],
        flops=200 << 20,
        moved=6 << 20,
    )(tab, got, win, w, spins)
    flat = lambda s, b: 2 * s + b
    other = lax.ppermute(oth, "box", [(0, 1), (1, 0)])
    down = [(flat(s, 0), s - 1) for s in range(1, n_samp)]
    up = [(flat(s, 1), s + 1) for s in range(n_samp - 1)]
    both = ("samp", "box")
    rim_a = lax.ppermute(
        rim_own, both, [(i, flat(s, 0)) for i, s in down] + [(i, flat(s, 1)) for i, s in up]
    )
    rim_b = lax.ppermute(
        rim_oth, both, [(i, flat(s, 1)) for i, s in down] + [(i, flat(s, 0)) for i, s in up]
    )
    (low,) = call(
        lower_kernel,
        [VMEM] * 4,
        [((64, 8, LANES), F32)],
        [
            pltpu.VMEM((2560, LANES), F32),
            pltpu.VMEM((2048, LANES), F32),
            pltpu.VMEM((LANES, 8, LANES), F32),
            pltpu.VMEM((32, LANES), I32),
            pltpu.SMEM((32, LANES), I32),
            dma,
        ],
        flops=20 << 20,
        moved=10 << 20,
    )(low_sources.T, low_operators.T, win, tab)
    low_incoming, high_incoming = call(
        final_kernel,
        [VMEM] * 7,
        [((512, LANES), F32), ((16, 2, 2, 512), F32)],
        [pltpu.VMEM((512, LANES), F32), pltpu.VMEM((16, 2, 2, 512), F32)]
        + [pltpu.VMEM((512, 768), BF16)] * 2
        + [dma((5,))],
        flops=300 << 20,
        moved=4 << 20,
        out_place=HBM,
    )(own, other, rim_a, rim_b, low.reshape(512, LANES), m, spins)
    return low_incoming.reshape(128, 2, 2, LANES), high_incoming


def solution(mesh):
    return jax.shard_map(
        shards,
        mesh=mesh,
        in_specs=(
            P(("box", "samp"), "rhs", None, None),
            P(("box", "rhs"), None, "samp"),
            P(("box", "rhs"), None, "samp"),
            P("box", None),
            P("box", None),
            P("box", None),
            P("box", None),
            P(),
            P(),
            P(),
        ),
        out_specs=(P("box", "rhs", None, "samp"), P("box", "rhs", None, "samp")),
        check_vma=False,
    )
```
